256 devices in a mesh: ctx: 8 (over y, z_hi), chan: 32 (over z_lo, x, core).
Axes of the slice: x: 4, y: 4, z: 8 (z_hi: 2, z_lo: 4; z = z_hi * 4 + z_lo), core: 2. Of those that a mesh axis runs over, the one named last changes fastest.
Arguments:
- inputs: bfloat16 [2048, 131072], P('chan', 'ctx'), may hold values from -6 to 6
- mixed: bfloat16 [2048, 131072], P('chan', 'ctx'), may hold values from -6 to 6
- grad_out: bfloat16 [2048, 131072], P('chan', 'ctx'), may hold values from -6 to 6
- left_weight: bfloat16 [256, 512, 512], P(('ctx', 'chan')), may hold values from -0.25 to 0.25
- right_weight: bfloat16 [512, 256, 256], P(('ctx', 'chan')), may hold values from -0.375 to 0.375
- first_weight: bfloat16 [32, 64, 64], replicated, may hold values from -0.75 to 0.75
- second_weight: bfloat16 [64, 32, 32], replicated, may hold values from -1 to 1
Outputs:
- grad_input: bfloat16 [2048, 131072], P('chan', 'ctx')
- grad_left: bfloat16 [256, 512, 512], P(('ctx', 'chan'))
- grad_right: bfloat16 [512, 256, 256], P(('ctx', 'chan'))
- grad_first: float32 [32, 64, 64], replicated
- grad_second: float32 [64, 32, 32], replicated
The draws below stay inside these ranges and needn't reach their ends.
All inputs are finite; a program needn't handle non-finite values.
Results may differ from the reference program's by a relative error of at most 0.0069.
Values may be sent and summed in bfloat16 or wider, within the bound.
A program may use at most 128 MiB of HBM per device.

```python
import jax
import jax.numpy as jnp
from jax import lax

CB = 64
CG = 32
BS = 512
NB = 256
D = 2048
SEQ = 131072


def levels(own_key, shape, pieces, low, top_value):
    def one(axis_at, shards_of):
        steps = jax.random.uniform(jax.random.fold_in(jax.random.fold_in(own_key, 6), axis_at), (shards_of,), jnp.float32, low / len(pieces), top_value / len(pieces))
        return jnp.repeat(jnp.exp(steps), shape[axis_at] // shards_of).reshape((-1,) + (1,) * (len(shape) - axis_at - 1))

    factor_of = one(*pieces[0])
    for cut in pieces[1:]:
        factor_of = factor_of * one(*cut)
    return factor_of


def bell_draw(own_key, extent, deviation, most, shards=(), dtype=jnp.bfloat16):
    drawn = deviation * jax.random.normal(own_key, extent, jnp.float32)
    if shards:
        drawn = drawn * levels(own_key, extent, shards, -0.22, 0.18)
    return jnp.clip(drawn, -most, most).astype(dtype)


def setup_inputs(seed: int = 0) -> dict:
    key_of = jax.random.split(jax.random.key(seed), 8)
    inputs = bell_draw(key_of[0], (D, SEQ), 1.0, 6.0, ((0, 32), (1, 8)))
    mixed = bell_draw(key_of[1], (D, SEQ), 1.0, 6.0, ((0, 32), (1, 8)))
    grad_out = bell_draw(key_of[2], (D, SEQ), 1.0, 6.0, ((0, 32), (1, 8)))
    left_weight = bell_draw(key_of[3], (NB, BS, BS), BS ** -0.5, 0.25, ((0, 256),))
    right_weight = bell_draw(key_of[4], (BS, NB, NB), NB ** -0.5, 0.375, ((0, 256),))
    first_weight = bell_draw(key_of[5], (CG, CB, CB), CB ** -0.5, 0.75)
    second_weight = bell_draw(key_of[6], (CB, CG, CG), CG ** -0.5, 1.0)
    return dict(inputs=inputs, mixed=mixed, grad_out=grad_out, left_weight=left_weight, right_weight=right_weight, first_weight=first_weight, second_weight=second_weight)


def lower_part(weight):
    size = weight.shape[-1]
    rows = lax.broadcasted_iota(jnp.int32, (size, size), 0)
    cols = lax.broadcasted_iota(jnp.int32, (size, size), 1)
    return jnp.where(rows >= cols, weight, jnp.zeros_like(weight))


def reference(inputs, mixed, grad_out, left_weight, right_weight, first_weight, second_weight):
    nblocks, bsize = left_weight.shape[0], left_weight.shape[1]
    width = inputs.shape[0]
    first32 = first_weight.astype(jnp.float32)
    second32 = second_weight.astype(jnp.float32)

    def blocks(arr):
        return jnp.transpose(arr.reshape(width, nblocks, bsize), (1, 2, 0))

    def channel_step(carry, parts):
        acc_first, acc_second = carry
        yblk, gblk = parts
        y4 = yblk.astype(jnp.float32).reshape(bsize, CG, CB)
        g4 = gblk.astype(jnp.float32).reshape(bsize, CG, CB)
        first_section = jnp.einsum("tgh,gkh->tgk", y4, first32).astype(jnp.bfloat16)
        section32 = first_section.astype(jnp.float32)
        gate_pre = jnp.einsum("tgk,kmg->tmk", section32, second32)
        sig = jax.nn.sigmoid(gate_pre)
        gate_grad = (g4 * y4 * sig * (1.0 + gate_pre * (1.0 - sig))).astype(jnp.bfloat16)
        gate32 = gate_grad.astype(jnp.float32)
        part_second = jnp.einsum("tmk,tgk->kmg", gate32, section32)
        first_grad = jnp.einsum("tmk,kmg->tgk", gate32, second32).astype(jnp.bfloat16)
        fgrad32 = first_grad.astype(jnp.float32)
        part_first = jnp.einsum("tgk,tgh->gkh", fgrad32, y4)
        mixed_grad = (g4 * gate_pre * sig + jnp.einsum("tgk,gkh->tgh", fgrad32, first32)).astype(jnp.bfloat16)
        return (acc_first + part_first, acc_second + part_second), mixed_grad.reshape(bsize, width)

    start = (jnp.zeros((CG, CB, CB), jnp.float32), jnp.zeros((CB, CG, CG), jnp.float32))
    (grad_first, grad_second), mixed_grad = lax.scan(channel_step, start, (blocks(mixed), blocks(grad_out)))

    piece = min(width, 128)
    count = width // piece
    mixed_grad = jnp.transpose(mixed_grad.reshape(nblocks, bsize, count, piece), (2, 3, 0, 1))
    lower_left = lower_part(left_weight).astype(jnp.float32)
    lower_right = lower_part(right_weight).astype(jnp.float32)

    def sequence_step(carry, parts):
        acc_left, acc_right = carry
        xc, dyc, gc = parts
        xc = xc.astype(jnp.float32)
        dyc = dyc.astype(jnp.float32)
        inner = jnp.einsum("ced,hcd->hce", lower_left, xc).astype(jnp.bfloat16).astype(jnp.float32)
        inner_grad = jnp.einsum("efc,hfe->hce", lower_right, dyc).astype(jnp.bfloat16).astype(jnp.float32)
        acc_right = acc_right + jnp.einsum("hfe,hce->efc", dyc, inner)
        result = (gc.astype(jnp.float32) + jnp.einsum("ced,hce->hcd", lower_left, inner_grad)).astype(jnp.bfloat16)
        acc_left = acc_left + jnp.einsum("hce,hcd->ced", inner_grad, xc)
        return (acc_left, acc_right), result

    start = (jnp.zeros((nblocks, bsize, bsize), jnp.float32), jnp.zeros((bsize, nblocks, nblocks), jnp.float32))
    shaped = (inputs.reshape(count, piece, nblocks, bsize), mixed_grad, grad_out.reshape(count, piece, nblocks, bsize))
    (acc_left, acc_right), result = lax.scan(sequence_step, start, shaped)
    grad_input = result.reshape(width, nblocks * bsize)
    grad_left = lower_part(acc_left).astype(jnp.bfloat16)
    grad_right = lower_part(acc_right).astype(jnp.bfloat16)
    return (grad_input, grad_left, grad_right, grad_first, grad_second)
```

```python
import functools

import jax
import jax.numpy as jnp
from jax import lax
from jax.experimental import pallas as pl
from jax.experimental.pallas import tpu as pltpu
from jax.sharding import PartitionSpec as P

MESH = pl.DeviceIdType.MESH
ANY = pl.BlockSpec(memory_space=pl.ANY)
NCTX, NCHAN, NDEV, HALF = 8, 32, 256, 16
BS, CB, CG, NB, D = 512, 64, 32, 256, 2048
KC = 16
F32, BF16 = jnp.float32, jnp.bfloat16


def coords():
    return lax.axis_index("ctx"), lax.axis_index("chan")


def chan_dev(chan):
    return (lax.axis_index("ctx"), chan)


def any_dev(linear):
    return (linear // NCHAN, lax.rem(linear, NCHAN))


def al(value, size):
    return pl.multiple_of(value * size, size)


def enter(count, device_of):
    barrier = pltpu.get_barrier_semaphore()

    @pl.loop(1, count)
    def _(step):
        pl.semaphore_signal(barrier, inc=1, device_id=device_of(step), device_id_type=MESH)

    pl.semaphore_wait(barrier, count - 1)


def remote(src, dst, send, recv, device):
    return pltpu.make_async_remote_copy(
        src_ref=src, dst_ref=dst, send_sem=send, recv_sem=recv, device_id=device, device_id_type=MESH
    )


def collect_kernel(
    x_ref, y_ref, g_ref, left_ref, xp_ref, yt_ref, gt_ref, lp_ref, send, recv, local
):
    ctx, me = coords()
    half, slot = me // HALF, lax.rem(me, HALF)
    partner = lax.rem(me + HALF, NCHAN)
    enter(NCHAN, lambda step: chan_dev(lax.rem(me + step, NCHAN)))

    def whole(src, dst, index, peer):
        return remote(
            src.at[:, pl.ds(al(peer, BS), BS)],
            dst.at[pl.ds(al(me, CB), CB), :],
            send.at[index],
            recv.at[index],
            chan_dev(peer),
        )

    def paired(part, other):
        return remote(
            x_ref.at[:, pl.ds(al(other + HALF * part, BS), BS)],
            xp_ref.at[part, pl.ds(al(slot, CB), CB), :],
            send.at[part],
            recv.at[part],
            chan_dev(half * HALF + other),
        )

    locals_ = [
        pltpu.make_async_copy(left_ref.at[0], lp_ref.at[half], local.at[0]),
        pltpu.make_async_copy(
            y_ref.at[:, pl.ds(al(me, BS), BS)], yt_ref.at[pl.ds(al(me, CB), CB), :], local.at[1]
        ),
        pltpu.make_async_copy(
            g_ref.at[:, pl.ds(al(me, BS), BS)], gt_ref.at[pl.ds(al(me, CB), CB), :], local.at[2]
        ),
    ]
    for part in range(2):
        locals_.append(
            pltpu.make_async_copy(
                x_ref.at[:, pl.ds(al(slot + HALF * part, BS), BS)],
                xp_ref.at[part, pl.ds(al(slot, CB), CB), :],
                local.at[3 + part],
            )
        )
    for copy in locals_:
        copy.start()
    left_copy = remote(left_ref.at[0], lp_ref.at[half], send.at[4], recv.at[4], chan_dev(partner))
    left_copy.start()

    @pl.loop(1, NCHAN)
    def _(step):
        whole(y_ref, yt_ref, 2, lax.rem(me + step, NCHAN)).start()

    @pl.loop(1, HALF)
    def _(step):
        other = lax.rem(slot + step, HALF)
        paired(0, other).start()
        paired(1, other).start()

    @pl.loop(1, NCHAN)
    def _(step):
        whole(g_ref, gt_ref, 3, lax.rem(me + step, NCHAN)).start()

    for copy in locals_:
        copy.wait()
    left_copy.wait()
    for part in range(2):
        area = xp_ref.at[part, pl.ds(0, (HALF - 1) * CB), :]
        remote(area, area, send.at[part], recv.at[part], chan_dev(partner)).wait()
    for index, dst in ((2, yt_ref), (3, gt_ref)):
        area = dst.at[pl.ds(0, (NCHAN - 1) * CB), :]
        remote(area, area, send.at[index], recv.at[index], chan_dev(partner)).wait()


def collect(x, y, g, left):
    return pl.pallas_call(
        collect_kernel,
        out_shape=[
            jax.ShapeDtypeStruct((2, HALF * CB, BS), BF16),
            jax.ShapeDtypeStruct((D, BS), BF16),
            jax.ShapeDtypeStruct((D, BS), BF16),
            jax.ShapeDtypeStruct((2, BS, BS), BF16),
        ],
        in_specs=[ANY] * 4,
        out_specs=[ANY] * 4,
        scratch_shapes=[
            pltpu.SemaphoreType.DMA((5,)),
            pltpu.SemaphoreType.DMA((5,)),
            pltpu.SemaphoreType.DMA((5,)),
        ],
        compiler_params=pltpu.CompilerParams(collective_id=1, has_side_effects=True),
        name="collect",
    )(x, y, g, left)


def linear_me():
    ctx, chan = coords()
    return ctx * NCHAN + chan


def plane_peer(step):
    ctx, chan = coords()
    y, z_hi, z_lo, xc = ctx // 2, lax.rem(ctx, 2), chan // 8, lax.rem(chan, 8)
    here = y * 8 + xc
    peer = lax.rem(here + step, 32)
    return here, peer, ((peer // 8) * 2 + z_hi, z_lo * 8 + lax.rem(peer, 8))


def column_peer(step):
    ctx, chan = coords()
    y, z_hi, z_lo, xc = ctx // 2, lax.rem(ctx, 2), chan // 8, lax.rem(chan, 8)
    here = z_hi * 4 + z_lo
    peer = lax.rem(here + step, 8)
    return here, peer, (y * 2 + peer // 4, lax.rem(peer, 4) * 8 + xc)


def everywhere(step):
    me = linear_me()
    peer = lax.rem(me + step, NDEV)
    return me, peer, any_dev(peer)


def exchange_kernel(groups, *refs):
    count = len(groups)
    srcs, dsts = refs[:count], refs[count : 2 * count]
    send, recv, local = refs[2 * count :]
    enter(NDEV, lambda step: everywhere(step)[2])

    def copy_of(index, step):
        here, peer, device = groups[index][1](step)
        return remote(
            srcs[index].at[peer], dsts[index].at[here], send.at[index], recv.at[index], device
        )

    locals_ = []
    for index, (_, peers) in enumerate(groups):
        here = peers(0)[0]
        locals_.append(
            pltpu.make_async_copy(srcs[index].at[here], dsts[index].at[here], local.at[index])
        )
    for copy in locals_:
        copy.start()
    for index, (size, _) in enumerate(groups):

        @pl.loop(1, size)
        def _(step, index=index):
            copy_of(index, step).start()

    for copy in locals_:
        copy.wait()
    for index, (size, peers) in enumerate(groups):
        area = dsts[index].at[pl.ds(0, size - 1)]
        remote(area, area, send.at[index], recv.at[index], peers(1)[2]).wait()


def exchange(arrays, groups, collective_id):
    count = len(arrays)
    return pl.pallas_call(
        functools.partial(exchange_kernel, groups),
        out_shape=[jax.ShapeDtypeStruct(a.shape, a.dtype) for a in arrays],
        in_specs=[ANY] * count,
        out_specs=[ANY] * count,
        scratch_shapes=[
            pltpu.SemaphoreType.DMA((count,)),
            pltpu.SemaphoreType.DMA((count,)),
            pltpu.SemaphoreType.DMA((count,)),
        ],
        compiler_params=pltpu.CompilerParams(collective_id=collective_id, has_side_effects=True),
        name="exchange",
    )(*arrays)


def give_back_kernel(ret_ref, grad_ref, term_ref, out_ref, got_ref, all_ref, send, recv, local):
    ctx, me = coords()
    half, slot = me // HALF, lax.rem(me, HALF)
    partner = lax.rem(me + HALF, NCHAN)
    here, _, _ = plane_peer(0)
    level, _, _ = column_peer(0)
    owned = here * 8 + level
    enter(NDEV, lambda step: everywhere(step)[2])

    def paired(part, other):
        return remote(
            ret_ref.at[part, pl.ds(al(other, CB), CB), :],
            out_ref.at[:, pl.ds(al(slot + HALF * part, BS), BS)],
            send.at[part],
            recv.at[part],
            chan_dev(half * HALF + other),
        )

    def shared(step):
        return remote(
            term_ref, all_ref.at[owned], send.at[3], recv.at[3], everywhere(step)[2]
        )

    locals_ = [pltpu.make_async_copy(term_ref, all_ref.at[owned], local.at[2])]
    for part in range(2):
        locals_.append(
            pltpu.make_async_copy(
                ret_ref.at[part, pl.ds(al(slot, CB), CB), :],
                out_ref.at[:, pl.ds(al(slot + HALF * part, BS), BS)],
                local.at[part],
            )
        )
    for copy in locals_:
        copy.start()
    grad_copy = remote(
        grad_ref.at[1 - half], got_ref, send.at[2], recv.at[2], chan_dev(partner)
    )
    grad_copy.start()

    @pl.loop(1, HALF)
    def _(step):
        other = lax.rem(slot + step, HALF)
        paired(0, other).start()
        paired(1, other).start()

    @pl.loop(1, NDEV)
    def _(step):
        shared(step).start()

    for copy in locals_:
        copy.wait()
    grad_copy.wait()
    for part in range(2):
        area = ret_ref.at[part, pl.ds(0, (HALF - 1) * CB), :]
        remote(area, area, send.at[part], recv.at[part], chan_dev(partner)).wait()
    area = all_ref.at[pl.ds(0, NDEV - 1)]
    remote(area, area, send.at[3], recv.at[3], chan_dev(partner)).wait()


def give_back(ret, grad, term):
    return pl.pallas_call(
        give_back_kernel,
        out_shape=[
            jax.ShapeDtypeStruct((CB, NCHAN * BS), BF16),
            jax.ShapeDtypeStruct((BS, BS), BF16),
            jax.ShapeDtypeStruct((NDEV, 8, 128), F32),
        ],
        in_specs=[ANY] * 3,
        out_specs=[ANY] * 3,
        scratch_shapes=[
            pltpu.SemaphoreType.DMA((4,)),
            pltpu.SemaphoreType.DMA((4,)),
            pltpu.SemaphoreType.DMA((3,)),
        ],
        compiler_params=pltpu.CompilerParams(collective_id=4, has_side_effects=True),
        name="give_back",
    )(ret, grad, term)


def dot(a, b, dims):
    return lax.dot_general(a, b, (dims, ((), ())), preferred_element_type=F32)


NN, NT, TN = ((1,), (0,)), ((1,), (1,)), ((0,), (0,))


def channel_kernel(
    y_ref, g_ref, w_ref, s_ref, eye_ref, pick_ref, mg_ref, pf_ref, ps_ref, fs, fg, gated
):
    for q in range(8):
        rows = pl.ds(q * 4, 4)
        fs[rows] = dot(w_ref[q], y_ref[rows].reshape(256, BS), NN).astype(BF16).reshape(4, CB, BS)
    for i in range(CB // KC):
        cols = pl.ds(i * KC, KC)
        s = s_ref[i]
        section = fs[:, cols, :].reshape(CG * KC, BS)
        pre = dot(s, section, NN)
        y = y_ref[:, cols, :].reshape(CG * KC, BS).astype(F32)
        g = g_ref[:, cols, :].reshape(CG * KC, BS).astype(F32)
        sig = jax.nn.sigmoid(pre)
        gsig = g * sig
        gg = (gsig * y * (1.0 + pre * (1.0 - sig))).astype(BF16)
        gated[:, cols, :] = (gsig * pre).reshape(CG, KC, BS)
        fg[:, cols, :] = dot(s, gg, TN).astype(BF16).reshape(CG, KC, BS)
        both = dot(gg, section, NT)
        row = lax.broadcasted_iota(jnp.int32, both.shape, 0)
        col = lax.broadcasted_iota(jnp.int32, both.shape, 1)
        both = jnp.where(lax.rem(row, KC) == lax.rem(col, KC), both, 0.0)
        ps_ref[i] = lax.dot_general(
            both,
            pick_ref[...],
            (NN, ((), ())),
            preferred_element_type=F32,
            precision=lax.Precision.HIGHEST,
        )
    for q in range(8):
        rows = pl.ds(q * 4, 4)
        fgq = fg[rows].reshape(256, BS)
        back = dot(w_ref[q], fgq, TN)
        mg = (gated[rows].reshape(256, BS) + back).astype(BF16)
        mg_ref[:, pl.ds(q * 256, 256)] = dot(eye_ref[...], mg, NT).astype(BF16)
        pf = dot(fgq, y_ref[rows].reshape(256, BS), NT)
        for a in range(4):
            pf_ref[q * 4 + a] = pf[a * CB : (a + 1) * CB, a * CB : (a + 1) * CB]


def channel(y, g, w, s, eye, pick):
    vmem = pl.BlockSpec(memory_space=pltpu.VMEM)
    return pl.pallas_call(
        channel_kernel,
        out_shape=[
            jax.ShapeDtypeStruct((BS, D), BF16),
            jax.ShapeDtypeStruct((CG, CB, CB), F32),
            jax.ShapeDtypeStruct((CB // KC, CG * KC, CG), F32),
        ],
        in_specs=[vmem] * 6,
        out_specs=[vmem] * 3,
        scratch_shapes=[
            pltpu.VMEM((CG, CB, BS), BF16),
            pltpu.VMEM((CG, CB, BS), BF16),
            pltpu.VMEM((CG, CB, BS), F32),
        ],
        compiler_params=pltpu.CompilerParams(vmem_limit_bytes=48 * 1024 * 1024),
        name="channel",
    )(y.reshape(CG, CB, BS), g.reshape(CG, CB, BS), w, s, eye, pick)


def lower_part(weight):
    size = weight.shape[-1]
    rows = lax.broadcasted_iota(jnp.int32, (size, size), 0)
    cols = lax.broadcasted_iota(jnp.int32, (size, size), 1)
    return jnp.where(rows >= cols, weight, jnp.zeros_like(weight))


def ein(spec, a, b):
    return jnp.einsum(spec, a, b, preferred_element_type=F32)


def on_device(inputs, mixed, grad_out, left_weight, right_weight, first_weight, second_weight):
    half = lax.axis_index("chan") // HALF
    eye4, eye16 = jnp.eye(4, dtype=BF16), jnp.eye(KC, dtype=BF16)
    w = (
        first_weight.reshape(8, 4, CB, 1, CB) * eye4[None, :, None, :, None]
    ).reshape(8, 4 * CB, 4 * CB)
    s = (
        second_weight.reshape(CB // KC, KC, CG, CG).transpose(0, 2, 1, 3)[..., None]
        * eye16[None, None, :, None, :]
    ).reshape(CB // KC, CG * KC, CG * KC)
    eye = jnp.eye(BS, dtype=BF16)
    pick = jnp.repeat(jnp.eye(CG, dtype=F32), KC, axis=0)

    xp, yt, gt, lp = collect(inputs, mixed, grad_out, left_weight)
    lower_left = lower_part(lp)
    mg, part_first, part_second = channel(yt, gt, w, s, eye, pick)
    inner = ein("sed,shd->seh", lower_left, xp).astype(BF16)
    inner_out = inner.reshape(2, NDEV, 2, HALF * CB).transpose(1, 0, 2, 3)
    part_second = part_second.reshape(CB // KC, CG, KC, CG).transpose(0, 2, 1, 3)
    parts = jnp.concatenate(
        [part_first.reshape(-1), part_second.reshape(-1), jnp.zeros((CB * CG * CG,), F32)]
    ).reshape(32, 8, 8, 128)
    mg_cols, inner_cols, parts = exchange(
        [mg.reshape(NDEV, 2, D), inner_out, parts],
        ((NDEV, everywhere), (NDEV, everywhere), (32, plane_peer)),
        2,
    )
    parts = jnp.sum(parts, axis=0)
    lower_right = lower_part(right_weight)
    inner_grad = ein("efc,feh->ceh", lower_right, mg_cols).astype(BF16)
    inner_cols = inner_cols.reshape(NCTX, 2, HALF, 2, 2, HALF * CB)
    inner_cols = inner_cols.transpose(4, 0, 3, 2, 1, 5).reshape(2, NB, D)
    grad_back = inner_grad.reshape(NCTX, 2, HALF, 2, 2, HALF * CB).transpose(0, 4, 2, 1, 3, 5)
    grad_back, parts = exchange(
        [grad_back.reshape(NDEV, 2, 2, HALF * CB), parts],
        ((NDEV, everywhere), (8, column_peer)),
        3,
    )
    grad_right = lower_part(ein("feh,ech->efc", mg_cols, inner_cols)).astype(BF16)
    parts = jnp.sum(parts, axis=0)
    grad_back = grad_back.transpose(1, 0, 2, 3).reshape(2, BS, HALF * CB)
    seq_term = ein("sed,seh->shd", lower_left, grad_back).astype(BF16)
    grad_left = ein("seh,shd->sed", grad_back, xp)
    seq_term, grad_other, parts = give_back(seq_term, grad_left.astype(BF16), parts)
    grad_input = (grad_out.astype(F32) + seq_term.astype(F32)).astype(BF16)
    own = lax.dynamic_index_in_dim(grad_left, half, 0, keepdims=False)
    grad_left = lower_part(own + grad_other.astype(F32)).astype(BF16)[None]
    parts = parts.reshape(-1)
    grad_first = parts[: CG * CB * CB].reshape(CG, CB, CB)
    grad_second = parts[CG * CB * CB : CG * CB * CB + CB * CG * CG].reshape(CB, CG, CG)
    return (grad_input, grad_left, grad_right, grad_first, grad_second)


def solution(mesh):
    in_specs = (
        P("chan", "ctx"),
        P("chan", "ctx"),
        P("chan", "ctx"),
        P(("ctx", "chan"), None, None),
        P(("ctx", "chan"), None, None),
        P(),
        P(),
    )
    out_specs = (
        P("chan", "ctx"),
        P(("ctx", "chan"), None, None),
        P(("ctx", "chan"), None, None),
        P(),
        P(),
    )
    return jax.shard_map(
        on_device, mesh=mesh, in_specs=in_specs, out_specs=out_specs, check_vma=False
    )
```

```python
import jax
import jax.numpy as jnp
from jax import lax
from jax.experimental import pallas as pl
from jax.experimental.pallas import tpu as pltpu
from jax.sharding import PartitionSpec as P

MESH = pl.DeviceIdType.MESH
ANY = pl.BlockSpec(memory_space=pl.ANY)
VMEM = pl.BlockSpec(memory_space=pltpu.VMEM)
NCTX, NCHAN, NDEV, HALF = 8, 32, 256, 16
BS, CB, CG, NB, D = 512, 64, 32, 256, 2048
KC = 16
F32, BF16 = jnp.float32, jnp.bfloat16
NN, NT, TN = ((1,), (0,)), ((1,), (1,)), ((0,), (0,))
LEFT, X0, X1, Y, G, RIGHT, IN0, IN1, MIX, PART1, IG0, IG1, GR, PART2, PART3, PART4, RET0, RET1, GL = range(19)
SEMS = 19


def dot(a, b, dims, precision=None):
    return lax.dot_general(a, b, (dims, ((), ())), preferred_element_type=F32, precision=precision)


def al(value, size):
    return pl.multiple_of(value * size, size)


def iota(shape, axis):
    return lax.broadcasted_iota(jnp.int32, shape, axis)


def kernel(
    x_ref, y_ref, g_ref, left_ref, right_ref, first_ref, second_ref,
    home_ref, gleft_ref, gright_ref, gfirst_ref, gsecond_ref,
    yt, gt, xp, lp, r16, inner, mg, mge, ine, parts, parts_in, part_own, part_col, part_sum, part_plane, part_all,
    ige, igx, gr, gr_in, ret, glp, glp_in,
    send, recv, local,
):
    ctx, chan = lax.axis_index("ctx"), lax.axis_index("chan")
    half, slot = chan // HALF, lax.rem(chan, HALF)
    yy, zhi, zlo, xc = ctx // 2, lax.rem(ctx, 2), chan // 8, lax.rem(chan, 8)
    me = ctx * NCHAN + chan
    group = ctx * 4 + zlo
    xq = lax.rem(xc, 4)
    inset = (xc // 4) == half
    partner = (ctx, lax.rem(chan + HALF, NCHAN))
    plane, level = yy * 8 + xc, zhi * 4 + zlo

    def linear_dev(linear):
        return (linear // NCHAN, lax.rem(linear, NCHAN))

    def remote(src, dst, index, device):
        return pltpu.make_async_remote_copy(
            src_ref=src, dst_ref=dst, send_sem=send.at[index], recv_sem=recv.at[index],
            device_id=device, device_id_type=MESH,
        )

    def finish(area, index):
        remote(area, area, index, partner).wait()

    def near(src, dst, index):
        return pltpu.make_async_copy(src, dst, local.at[index])

    barrier = pltpu.get_barrier_semaphore()

    @pl.loop(1, NDEV)
    def _(step):
        pl.semaphore_signal(
            barrier, inc=1, device_id=linear_dev(lax.rem(me + step, NDEV)), device_id_type=MESH
        )

    pl.semaphore_wait(barrier, NDEV - 1)

    def paired(part, other):
        return (
            x_ref.at[:, pl.ds(al(other + HALF * part, BS), BS)],
            xp.at[part, pl.ds(al(slot, CB), CB), :],
        )

    def whole(src, dst, peer):
        return src.at[:, pl.ds(al(peer, BS), BS)], dst.at[pl.ds(al(chan, CB), CB), :]

    remote(left_ref.at[0], lp.at[half], LEFT, partner).start()
    begin = [
        near(left_ref.at[0], lp.at[half], LEFT),
        near(*paired(0, slot), X0),
        near(*paired(1, slot), X1),
        near(*whole(y_ref, yt, chan), Y),
        near(*whole(g_ref, gt, chan), G),
        near(right_ref, r16.at[pl.ds(xc * 2, 2)], RIGHT),
    ]
    for copy in begin:
        copy.start()

    @pl.loop(1, HALF)
    def _(step):
        other = lax.rem(slot + step, HALF)
        for part in range(2):
            remote(*paired(part, other), X0 + part, (ctx, half * HALF + other)).start()

    @pl.loop(1, NCHAN)
    def _(step):
        peer = lax.rem(chan + step, NCHAN)
        remote(*whole(y_ref, yt, peer), Y, (ctx, peer)).start()

    @pl.loop(1, NCHAN)
    def _(step):
        peer = lax.rem(chan + step, NCHAN)
        remote(*whole(g_ref, gt, peer), G, (ctx, peer)).start()

    @pl.loop(1, 8)
    def _(step):
        peer = lax.rem(xc + step, 8)
        remote(right_ref, r16.at[pl.ds(xc * 2, 2)], RIGHT, (ctx, zlo * 8 + peer)).start()

    for copy in begin:
        copy.wait()

    finish(lp.at[0], LEFT)
    for part in range(2):
        finish(xp.at[part, pl.ds(0, (HALF - 1) * CB), :], X0 + part)
    keep = iota((BS, BS), 0) >= iota((BS, BS), 1)
    for part in range(2):
        lower = jnp.where(keep, lp[part], jnp.zeros((BS, BS), BF16))
        lp[part] = lower
        inner[part] = dot(lower, xp[part], NT).astype(BF16)

    def inner_to(part, other_group, quarter):
        src = inner.at[part, pl.ds(al(other_group, 16), 16), pl.ds(al(quarter, 256), 256)]
        dst = ine.at[ctx * NCHAN + slot + HALF * part]
        return src, dst, (other_group // 4, lax.rem(other_group, 4) * 8 + half * 4 + quarter)

    def channel(w, s, fs, fg, gated):
        rows4, cols4 = iota((256, 256), 0), iota((256, 256), 1)
        same = (rows4 // CB) == (cols4 // CB)
        spread4 = (lax.rem(iota((CB, 256), 1), CB) == iota((CB, 256), 0)).astype(BF16)
        for q in range(8):
            tall = first_ref[pl.ds(q * 4, 4)].reshape(256, CB)
            w[q] = jnp.where(same, dot(tall, spread4, NN), 0.0).astype(BF16)
        spread16 = (iota((CG, BS), 1) // KC == iota((CG, BS), 0)).astype(BF16)
        row, col = iota((BS, BS), 0), iota((BS, BS), 1)
        perm = (lax.rem(row, KC) * CG + row // KC == col).astype(BF16)
        for i in range(CB // KC):
            tall = second_ref[pl.ds(i * KC, KC)].reshape(BS, CG)
            wide = jnp.where(row // CG == lax.rem(col, KC), dot(tall, spread16, NN), 0.0)
            s[i] = dot(perm, wide.astype(BF16), NN).astype(BF16)

        finish(yt.at[pl.ds(0, (NCHAN - 1) * CB), :], Y)
        for q in range(8):
            section = dot(w[q], yt[pl.ds(q * 256, 256), :], NN).astype(BF16)
            fs[pl.ds(q * 4, 4)] = section.reshape(4, CB, BS)
        finish(gt.at[pl.ds(0, (NCHAN - 1) * CB), :], G)

        @pl.when(inset)
        def _():
            for part in range(2):
                src, dst, _ = inner_to(part, group, xq)
                near(src, dst, IN0 + part).start()

        @pl.when(jnp.logical_not(inset))
        def _():
            for part in range(2):
                src, dst, device = inner_to(part, group, xq)
                remote(src, dst, IN0 + part, device).start()

        @pl.loop(1, 128)
        def _(step):
            for part in range(2):
                src, dst, device = inner_to(
                    part, lax.rem(group + step // 4, 32), lax.rem(xq + step, 4)
                )
                remote(src, dst, IN0 + part, device).start()

        y3, g3 = yt.reshape(CG, CB, BS), gt.reshape(CG, CB, BS)
        lane = iota((BS, 128), 1)
        source = iota((BS, 128), 0) // KC
        second = jnp.zeros((BS, 128), F32)
        for i in range(CB // KC):
            cols = pl.ds(i * KC, KC)
            section = fs[:, cols, :].reshape(BS, BS)
            pre = dot(s[i], section, NN)
            y = y3[:, cols, :].reshape(BS, BS).astype(F32)
            g = g3[:, cols, :].reshape(BS, BS).astype(F32)
            sig = jax.nn.sigmoid(pre)
            gsig = g * sig
            gg = (gsig * y * (1.0 + pre * (1.0 - sig))).astype(BF16)
            gated[:, cols, :] = (gsig * pre).reshape(CG, KC, BS)
            fg[:, cols, :] = dot(s[i], gg, TN).astype(BF16).reshape(CG, KC, BS)
            both = dot(gg, section, NT)
            both = jnp.where(lax.rem(row, KC) == lax.rem(col, KC), both, 0.0)
            pick = (lane == source + CG * i).astype(F32)
            second += dot(both, pick, NN, lax.Precision.HIGHEST)
        parts[pl.ds(1024, 512), :] = second
        parts[pl.ds(1536, 512), :] = jnp.zeros((512, 128), F32)
        eye = (row == col).astype(BF16)
        left_lane = iota((CB, 128), 1) < CB
        for q in range(8):
            quad = pl.ds(q * 4, 4)
            fgq = fg[quad].reshape(256, BS)
            back = dot(w[q], fgq, TN)
            grad = (gated[quad].reshape(256, BS) + back).astype(BF16)
            mg[:, pl.ds(q * 256, 256)] = dot(eye, grad, NT).astype(BF16)
            pf = dot(fgq, yt[pl.ds(q * 256, 256), :], NT)
            for a in range(2):
                one = pf[a * 128 : a * 128 + CB, a * 128 : a * 128 + 128]
                two = pf[a * 128 + CB : a * 128 + 128, a * 128 : a * 128 + 128]
                parts[pl.ds((q * 2 + a) * CB, CB), :] = jnp.where(left_lane, one, two)

    pl.run_scoped(
        channel,
        pltpu.VMEM((8, 256, 256), BF16),
        pltpu.VMEM((CB // KC, BS, BS), BF16),
        pltpu.VMEM((CG, CB, BS), BF16),
        pltpu.VMEM((CG, CB, BS), BF16),
        pltpu.VMEM((CG, CB, BS), F32),
    )

    def mixed_to(peer):
        return mg.at[pl.ds(al(peer // 8, 16), 16), pl.ds(al(lax.rem(peer, 8), 256), 256)], mge.at[me]

    near(*mixed_to(me), MIX).start()

    @pl.loop(1, NDEV)
    def _(step):
        peer = lax.rem(me + step, NDEV)
        remote(*mixed_to(peer), MIX, linear_dev(peer)).start()

    def plane_dev(peer):
        return ((peer // 8) * 2 + zhi, zlo * 8 + lax.rem(peer, 8))

    def column_dev(peer):
        return (yy * 2 + peer // 4, lax.rem(peer, 4) * 8 + xc)

    def share(peer):
        return parts.at[pl.ds(al(peer, 64), 64), :], parts_in.at[plane]

    near(*share(plane), PART1).start()

    @pl.loop(1, 32)
    def _(step):
        peer = lax.rem(plane + step, 32)
        remote(*share(peer), PART1, plane_dev(peer)).start()

    near(*share(plane), PART1).wait()
    finish(parts_in.at[pl.ds(0, 31)], PART1)
    part_own[...] = jnp.sum(parts_in[...], axis=0)

    def column_share(peer):
        return part_own.at[pl.ds(al(peer, 8), 8), :], part_col.at[level]

    near(*column_share(level), PART2).start()

    @pl.loop(1, 8)
    def _(step):
        peer = lax.rem(level + step, 8)
        remote(*column_share(peer), PART2, column_dev(peer)).start()

    keep_right = iota((NB, NB), 0) >= iota((NB, NB), 1)
    finish(r16.at[pl.ds(0, 14)], RIGHT)

    def back_to(part, other_ctx, other_slot):
        src = ige.at[other_ctx * NCHAN + other_slot + HALF * part]
        dst = igx.at[part, pl.ds(al(group, 16), 16), pl.ds(al(xq, 256), 256)]
        return src, dst, (other_ctx, (xc // 4) * HALF + other_slot)

    def columns(wide0, wide1, mge_by):
        wide = (wide0, wide1)

        def unpack(ref):
            for j in range(2):
                lanes = pl.ds(j * 128, 128)
                wide[j][...] = ref[:, :, lanes].reshape(NB * 16, 128).astype(F32)

        def take(e):
            rows = pl.ds(e, NB, stride=16)
            return jnp.concatenate([w[rows, :] for w in wide], axis=1).astype(BF16)

        near(*mixed_to(me), MIX).wait()
        finish(mge.at[pl.ds(0, NDEV - 1)], MIX)
        unpack(mge)

        @pl.loop(0, 16)
        def _(e):
            mge_by[e] = take(e)

        @pl.loop(0, 16)
        def _(e):
            lower = jnp.where(keep_right, r16[e], jnp.zeros((NB, NB), BF16))
            one = dot(lower, mge_by[e], TN)
            for j in range(2):
                wide[j][pl.ds(e, NB, stride=16), :] = one[:, j * 128 : (j + 1) * 128]

        for j in range(2):
            lanes = pl.ds(j * 128, 128)
            ige[:, :, lanes] = wide[j][...].astype(BF16).reshape(NB, 16, 128)

        @pl.when(inset)
        def _():
            for part in range(2):
                src, dst, _ = back_to(part, ctx, slot)
                near(src, dst, IG0 + part).start()

        @pl.when(jnp.logical_not(inset))
        def _():
            for part in range(2):
                src, dst, device = back_to(part, ctx, slot)
                remote(src, dst, IG0 + part, device).start()

        @pl.loop(1, 128)
        def _(step):
            for part in range(2):
                src, dst, device = back_to(
                    part, lax.rem(ctx + step // HALF, NCTX), lax.rem(slot + step, HALF)
                )
                remote(src, dst, IG0 + part, device).start()

        near(*column_share(level), PART2).wait()
        finish(part_col.at[pl.ds(0, 7)], PART2)
        part_sum[...] = jnp.sum(part_col[...], axis=0)
        near(part_sum, part_plane.at[level], PART3).start()

        @pl.loop(1, 8)
        def _(step):
            peer = lax.rem(level + step, 8)
            remote(part_sum, part_plane.at[level], PART3, column_dev(peer)).start()

        @pl.when(inset)
        def _():
            for part in range(2):
                src, dst, _ = inner_to(part, group, xq)
                near(src, dst, IN0 + part).wait()
                finish(ine.at[pl.ds(0, 127)], IN0 + part)

        @pl.when(jnp.logical_not(inset))
        def _():
            for part in range(2):
                finish(ine.at[pl.ds(0, 128)], IN0 + part)

        unpack(ine)

        @pl.loop(0, 16)
        def _(e):
            one = dot(mge_by[e], take(e), NT)
            gr[e] = jnp.where(keep_right, one, 0.0).astype(BF16)

    pl.run_scoped(
        columns,
        pltpu.VMEM((NB * 16, 128), F32),
        pltpu.VMEM((NB * 16, 128), F32),
        pltpu.VMEM((16, NB, 256), BF16),
    )

    def right_to(peer):
        return gr.at[pl.ds(peer * 2, 2)], gr_in.at[xc]

    near(*right_to(xc), GR).start()

    @pl.loop(1, 8)
    def _(step):
        peer = lax.rem(xc + step, 8)
        remote(*right_to(peer), GR, (ctx, zlo * 8 + peer)).start()

    near(part_sum, part_plane.at[level], PART3).wait()
    finish(part_plane.at[pl.ds(0, 7)], PART3)
    near(part_plane, part_all.at[plane], PART4).start()

    @pl.loop(1, 32)
    def _(step):
        peer = lax.rem(plane + step, 32)
        remote(part_plane, part_all.at[plane], PART4, plane_dev(peer)).start()

    @pl.when(inset)
    def _():
        for part in range(2):
            src, dst, _ = back_to(part, ctx, slot)
            near(src, dst, IG0 + part).wait()
            finish(ige.at[pl.ds(0, 127)], IG0 + part)

    @pl.when(jnp.logical_not(inset))
    def _():
        for part in range(2):
            finish(ige.at[pl.ds(0, 128)], IG0 + part)

    def home_to(part, other):
        return (
            ret.at[part, pl.ds(al(other, CB), CB), :],
            home_ref.at[:, pl.ds(al(slot + HALF * part, BS), BS)],
        )

    for part in range(2):
        ret[part] = dot(igx[part], lp[part], TN).astype(BF16)
        near(*home_to(part, slot), RET0 + part).start()

        @pl.loop(1, HALF)
        def _(step, part=part):
            other = lax.rem(slot + step, HALF)
            remote(*home_to(part, other), RET0 + part, (ctx, half * HALF + other)).start()

    glp[...] = dot(igx[1 - half], xp[1 - half], NN).astype(BF16)
    remote(glp, glp_in, GL, partner).start()
    own = dot(igx[half], xp[half], NN)

    near(part_plane, part_all.at[plane], PART4).wait()
    finish(part_all.at[pl.ds(0, 31)], PART4)
    flat = part_all.reshape(NB * 8, 128)
    for p in range(16):
        block = flat[pl.ds(p * CB, CB), :]
        gfirst_ref[2 * p] = block[:, :CB]
        gfirst_ref[2 * p + 1] = block[:, CB:]
    for k in range(KC):
        block = flat[pl.ds(1024 + k, CG, stride=KC), :]
        for i in range(CB // KC):
            gsecond_ref[i * KC + k] = block[:, i * CG : (i + 1) * CG]

    near(*right_to(xc), GR).wait()
    finish(gr_in.at[pl.ds(0, 7)], GR)
    total = gr_in[0].astype(F32)
    for other in range(1, 8):
        total += gr_in[other].astype(F32)
    gright_ref[...] = total.astype(BF16)

    finish(glp_in, GL)
    gleft_ref[0] = jnp.where(keep, own + glp_in[...].astype(F32), 0.0).astype(BF16)
    for part in range(2):
        near(*home_to(part, slot), RET0 + part).wait()
        finish(ret.at[part, pl.ds(0, (HALF - 1) * CB), :], RET0 + part)


def on_device(inputs, mixed, grad_out, left_weight, right_weight, first_weight, second_weight):
    home, grad_left, grad_right, grad_first, grad_second = pl.pallas_call(
        kernel,
        out_shape=[
            jax.ShapeDtypeStruct((CB, NCHAN * BS), BF16),
            jax.ShapeDtypeStruct((1, BS, BS), BF16),
            jax.ShapeDtypeStruct((2, NB, NB), BF16),
            jax.ShapeDtypeStruct((CG, CB, CB), F32),
            jax.ShapeDtypeStruct((CB, CG, CG), F32),
        ],
        in_specs=[ANY] * 5 + [VMEM] * 2,
        out_specs=[ANY] + [VMEM] * 4,
        scratch_shapes=[
            pltpu.VMEM((D, BS), BF16),
            pltpu.VMEM((D, BS), BF16),
            pltpu.VMEM((2, HALF * CB, BS), BF16),
            pltpu.VMEM((2, BS, BS), BF16),
            pltpu.VMEM((16, NB, NB), BF16),
            pltpu.VMEM((2, BS, HALF * CB), BF16),
            pltpu.VMEM((BS, D), BF16),
            pltpu.VMEM((NB, 16, 256), BF16),
            pltpu.VMEM((NB, 16, 256), BF16),
            pltpu.VMEM((2048, 128), F32),
            pltpu.VMEM((32, 64, 128), F32),
            pltpu.VMEM((64, 128), F32),
            pltpu.VMEM((8, 8, 128), F32),
            pltpu.VMEM((8, 128), F32),
            pltpu.VMEM((8, 8, 128), F32),
            pltpu.VMEM((32, 8, 8, 128), F32),
            pltpu.VMEM((NB, 16, 256), BF16),
            pltpu.VMEM((2, BS, HALF * CB), BF16),
            pltpu.VMEM((16, NB, NB), BF16),
            pltpu.VMEM((8, 2, NB, NB), BF16),
            pltpu.VMEM((2, HALF * CB, BS), BF16),
            pltpu.VMEM((BS, BS), BF16),
            pltpu.VMEM((BS, BS), BF16),
            pltpu.SemaphoreType.DMA((SEMS,)),
            pltpu.SemaphoreType.DMA((SEMS,)),
            pltpu.SemaphoreType.DMA((SEMS,)),
        ],
        compiler_params=pltpu.CompilerParams(
            collective_id=1, has_side_effects=True, vmem_limit_bytes=62 * 1024 * 1024
        ),
        name="layer",
    )(inputs, mixed, grad_out, left_weight, right_weight, first_weight, second_weight)
    grad_input = (grad_out.astype(F32) + home.astype(F32)).astype(BF16)
    return (grad_input, grad_left, grad_right, grad_first, grad_second)


def solution(mesh):
    in_specs = (
        P("chan", "ctx"),
        P("chan", "ctx"),
        P("chan", "ctx"),
        P(("ctx", "chan"), None, None),
        P(("ctx", "chan"), None, None),
        P(),
        P(),
    )
    out_specs = (
        P("chan", "ctx"),
        P(("ctx", "chan"), None, None),
        P(("ctx", "chan"), None, None),
        P(),
        P(),
    )
    return jax.shard_map(
        on_device, mesh=mesh, in_specs=in_specs, out_specs=out_specs, check_vma=False
    )
```

```python
import jax
import jax.numpy as jnp
from jax import lax
from jax.experimental import pallas as pl
from jax.experimental.pallas import tpu as pltpu
from jax.sharding import PartitionSpec as P

MESH = pl.DeviceIdType.MESH
ANY = pl.BlockSpec(memory_space=pl.ANY)
VMEM = pl.BlockSpec(memory_space=pltpu.VMEM)
NCTX, NCHAN, NDEV, HALF = 8, 32, 256, 16
BS, CB, CG, NB, D = 512, 64, 32, 256, 2048
KC = 16
F32, BF16 = jnp.float32, jnp.bfloat16
NN, NT, TN = ((1,), (0,)), ((1,), (1,)), ((0,), (0,))
LEFT, X0, X1, Y, G, RIGHT, IN0, IN1, MIX, PART1, IG0, IG1, GR, PART2, PART3, PART4, RET0, RET1, GL = range(19)
SEMS = 19


def dot(a, b, dims, precision=None):
    return lax.dot_general(a, b, (dims, ((), ())), preferred_element_type=F32, precision=precision)


def al(value, size):
    return pl.multiple_of(value * size, size)


def iota(shape, axis):
    return lax.broadcasted_iota(jnp.int32, shape, axis)


def kernel(
    x_ref, y_ref, g_ref, left_ref, right_ref, first_ref, second_ref,
    home_ref, gleft_ref, gright_ref, gfirst_ref, gsecond_ref,
    yt, gt, xp, lp, r16, inner, mg, mge, ine, parts, parts_in, part_own, part_col, part_sum, part_plane, part_all,
    ige, igx, gr, gr_in, ret, glp, glp_in,
    send, recv, local, ready,
):
    ctx, chan = lax.axis_index("ctx"), lax.axis_index("chan")
    half, slot = chan // HALF, lax.rem(chan, HALF)
    yy, zhi, zlo, xc = ctx // 2, lax.rem(ctx, 2), chan // 8, lax.rem(chan, 8)
    me = ctx * NCHAN + chan
    group = ctx * 4 + zlo
    xq = lax.rem(xc, 4)
    inset = (xc // 4) == half
    partner = (ctx, lax.rem(chan + HALF, NCHAN))
    plane, level = yy * 8 + xc, zhi * 4 + zlo

    def linear_dev(linear):
        return (linear // NCHAN, lax.rem(linear, NCHAN))

    def remote(src, dst, index, device):
        return pltpu.make_async_remote_copy(
            src_ref=src, dst_ref=dst, send_sem=send.at[index], recv_sem=recv.at[index],
            device_id=device, device_id_type=MESH,
        )

    def finish(area, index):
        remote(area, area, index, partner).wait()

    def near(src, dst, index):
        return pltpu.make_async_copy(src, dst, local.at[index])

    barrier = pltpu.get_barrier_semaphore()

    def greet(semaphore, count, device_of):
        @pl.loop(1, count)
        def _(step):
            pl.semaphore_signal(
                semaphore, inc=1, device_id=device_of(step), device_id_type=MESH
            )

    def across(step):
        return (lax.rem(ctx + step, NCTX), chan)

    greet(barrier, NCHAN, lambda step: (ctx, lax.rem(chan + step, NCHAN)))
    greet(barrier, NCTX, across)
    pl.semaphore_wait(barrier, NCHAN + NCTX - 2)
    greet(ready, NCTX, across)

    def paired(part, other):
        return (
            x_ref.at[:, pl.ds(al(other + HALF * part, BS), BS)],
            xp.at[part, pl.ds(al(slot, CB), CB), :],
        )

    def whole(src, dst, peer):
        return src.at[:, pl.ds(al(peer, BS), BS)], dst.at[pl.ds(al(chan, CB), CB), :]

    def bands(src, dst, index):
        for band in range(4):
            area = (pl.ds(band * 128, 128), pl.ds(0, band * 128 + 128))
            remote(src.at[area], dst.at[area], index, partner).start()

    bands(left_ref.at[0], lp.at[half], LEFT)
    begin = [
        near(left_ref.at[0], lp.at[half], LEFT),
        near(*paired(0, slot), X0),
        near(*paired(1, slot), X1),
        near(*whole(y_ref, yt, chan), Y),
        near(*whole(g_ref, gt, chan), G),
        near(right_ref, r16.at[pl.ds(xc * 2, 2)], RIGHT),
    ]
    for copy in begin:
        copy.start()

    @pl.loop(1, NCHAN)
    def _(step):
        peer = lax.rem(chan + step * 11, NCHAN)
        remote(*whole(y_ref, yt, peer), Y, (ctx, peer)).start()

        @pl.when(step < HALF)
        def _():
            other = lax.rem(slot + step, HALF)
            for part in range(2):
                remote(*paired(part, other), X0 + part, (ctx, half * HALF + other)).start()

    @pl.loop(1, NCHAN)
    def _(step):
        peer = lax.rem(chan + step * 11, NCHAN)
        remote(*whole(g_ref, gt, peer), G, (ctx, peer)).start()

        @pl.when(step < 8)
        def _():
            other = lax.rem(xc + step, 8)
            remote(right_ref, r16.at[pl.ds(xc * 2, 2)], RIGHT, (ctx, zlo * 8 + other)).start()

    for copy in begin:
        copy.wait()

    finish(lp.at[0, pl.ds(0, 320), :], LEFT)
    for part in range(2):
        finish(xp.at[part, pl.ds(0, (HALF - 1) * CB), :], X0 + part)
    keep = iota((BS, BS), 0) >= iota((BS, BS), 1)
    for part in range(2):
        lower = jnp.where(keep, lp[part], jnp.zeros((BS, BS), BF16))
        lp[part] = lower
        inner[part] = dot(lower, xp[part], NT).astype(BF16)

    def inner_to(part, other_group, quarter):
        src = inner.at[part, pl.ds(al(other_group, 16), 16), pl.ds(al(quarter, 256), 256)]
        dst = ine.at[ctx * NCHAN + slot + HALF * part]
        return src, dst, (other_group // 4, lax.rem(other_group, 4) * 8 + half * 4 + quarter)

    def inner_send(part):
        @pl.when(inset)
        def _():
            src, dst, _ = inner_to(part, group, xq)
            near(src, dst, IN0 + part).start()

        @pl.when(jnp.logical_not(inset))
        def _():
            src, dst, device = inner_to(part, group, xq)
            remote(src, dst, IN0 + part, device).start()

        @pl.loop(1, 128)
        def _(step):
            src, dst, device = inner_to(
                part, lax.rem(group + step // 4, 32), lax.rem(xq + step, 4)
            )
            remote(src, dst, IN0 + part, device).start()

    def channel(w, s, fs, fg, gated):
        rows4, cols4 = iota((256, 256), 0), iota((256, 256), 1)
        same = (rows4 // CB) == (cols4 // CB)
        spread4 = (lax.rem(iota((CB, 256), 1), CB) == iota((CB, 256), 0)).astype(BF16)
        for q in range(8):
            tall = first_ref[pl.ds(q * 4, 4)].reshape(256, CB)
            w[q] = jnp.where(same, dot(tall, spread4, NN), 0.0).astype(BF16)
        spread16 = (iota((CG, BS), 1) // KC == iota((CG, BS), 0)).astype(BF16)
        row, col = iota((BS, BS), 0), iota((BS, BS), 1)
        perm = (lax.rem(row, KC) * CG + row // KC == col).astype(BF16)
        for i in range(CB // KC):
            tall = second_ref[pl.ds(i * KC, KC)].reshape(BS, CG)
            wide = jnp.where(row // CG == lax.rem(col, KC), dot(tall, spread16, NN), 0.0)
            s[i] = dot(perm, wide.astype(BF16), NN).astype(BF16)

        finish(yt.at[pl.ds(0, (NCHAN - 1) * CB), :], Y)
        for q in range(8):
            section = dot(w[q], yt[pl.ds(q * 256, 256), :], NN).astype(BF16)
            fs[pl.ds(q * 4, 4)] = section.reshape(4, CB, BS)
        finish(gt.at[pl.ds(0, (NCHAN - 1) * CB), :], G)

        pl.semaphore_wait(ready, NCTX - 1)
        inner_send(0)
        y3, g3 = yt.reshape(CG, CB, BS), gt.reshape(CG, CB, BS)
        lane = iota((BS, 128), 1)
        source = iota((BS, 128), 0) // KC
        second = jnp.zeros((BS, 128), F32)
        for i in range(CB // KC):
            cols = pl.ds(i * KC, KC)
            section = fs[:, cols, :].reshape(BS, BS)
            pre = dot(s[i], section, NN)
            y = y3[:, cols, :].reshape(BS, BS).astype(F32)
            g = g3[:, cols, :].reshape(BS, BS).astype(F32)
            sig = jax.nn.sigmoid(pre)
            gsig = g * sig
            gg = (gsig * y * (1.0 + pre * (1.0 - sig))).astype(BF16)
            gated[:, cols, :] = (gsig * pre).reshape(CG, KC, BS)
            fg[:, cols, :] = dot(s[i], gg, TN).astype(BF16).reshape(CG, KC, BS)
            both = dot(gg, section, NT)
            both = jnp.where(lax.rem(row, KC) == lax.rem(col, KC), both, 0.0)
            pick = (lane == source + CG * i).astype(F32)
            second += dot(both, pick, NN, lax.Precision.HIGHEST)
        parts[pl.ds(1024, 512), :] = second
        parts[pl.ds(1536, 512), :] = jnp.zeros((512, 128), F32)
        eye = (row == col).astype(BF16)
        left_lane = iota((CB, 128), 1) < CB
        for q in range(8):
            quad = pl.ds(q * 4, 4)
            fgq = fg[quad].reshape(256, BS)
            back = dot(w[q], fgq, TN)
            grad = (gated[quad].reshape(256, BS) + back).astype(BF16)
            mg[:, pl.ds(q * 256, 256)] = dot(eye, grad, NT).astype(BF16)
            pf = dot(fgq, yt[pl.ds(q * 256, 256), :], NT)
            for a in range(2):
                one = pf[a * 128 : a * 128 + CB, a * 128 : a * 128 + 128]
                two = pf[a * 128 + CB : a * 128 + 128, a * 128 : a * 128 + 128]
                parts[pl.ds((q * 2 + a) * CB, CB), :] = jnp.where(left_lane, one, two)

    pl.run_scoped(
        channel,
        pltpu.VMEM((8, 256, 256), BF16),
        pltpu.VMEM((CB // KC, BS, BS), BF16),
        pltpu.VMEM((CG, CB, BS), BF16),
        pltpu.VMEM((CG, CB, BS), BF16),
        pltpu.VMEM((CG, CB, BS), F32),
    )

    def mixed_to(peer):
        return mg.at[pl.ds(al(peer // 8, 16), 16), pl.ds(al(lax.rem(peer, 8), 256), 256)], mge.at[me]

    near(*mixed_to(me), MIX).start()

    @pl.loop(1, NDEV)
    def _(step):
        peer = lax.rem(me + step, NDEV)
        remote(*mixed_to(peer), MIX, linear_dev(peer)).start()

    def plane_dev(peer):
        return ((peer // 8) * 2 + zhi, zlo * 8 + lax.rem(peer, 8))

    def column_dev(peer):
        return (yy * 2 + peer // 4, lax.rem(peer, 4) * 8 + xc)

    def share(peer):
        return parts.at[pl.ds(al(peer, 64), 64), :], parts_in.at[plane]

    near(*share(plane), PART1).start()

    @pl.loop(1, 32)
    def _(step):
        peer = lax.rem(plane + step, 32)
        remote(*share(peer), PART1, plane_dev(peer)).start()

    inner_send(1)
    near(*share(plane), PART1).wait()
    finish(parts_in.at[pl.ds(0, 31)], PART1)
    part_own[...] = jnp.sum(parts_in[...], axis=0)

    def column_share(peer):
        return part_own.at[pl.ds(al(peer, 8), 8), :], part_col.at[level]

    near(*column_share(level), PART2).start()

    @pl.loop(1, 8)
    def _(step):
        peer = lax.rem(level + step, 8)
        remote(*column_share(peer), PART2, column_dev(peer)).start()

    keep_right = iota((NB, NB), 0) >= iota((NB, NB), 1)
    finish(r16.at[pl.ds(0, 14)], RIGHT)

    @pl.loop(0, 16)
    def _(e):
        r16[e] = jnp.where(keep_right, r16[e], jnp.zeros((NB, NB), BF16)).T

    def back_to(part, other_ctx, other_slot):
        src = ige.at[other_ctx * NCHAN + other_slot + HALF * part]
        dst = igx.at[part, pl.ds(al(group, 16), 16), pl.ds(al(xq, 256), 256)]
        return src, dst, (other_ctx, (xc // 4) * HALF + other_slot)

    def columns(wide0, wide1, mge_by):
        wide = (wide0, wide1)

        def unpack(ref):
            for j in range(2):
                lanes = pl.ds(j * 128, 128)
                wide[j][...] = ref[:, :, lanes].reshape(NB * 16, 128).astype(F32)

        def take(e):
            rows = pl.ds(e, NB, stride=16)
            return jnp.concatenate([w[rows, :] for w in wide], axis=1).astype(BF16)

        near(*mixed_to(me), MIX).wait()
        finish(mge.at[pl.ds(0, NDEV - 1)], MIX)
        unpack(mge)

        @pl.loop(0, 16)
        def _(e):
            mge_by[e] = take(e)

        @pl.loop(0, 16)
        def _(e):
            one = dot(r16[e], mge_by[e], NN)
            for j in range(2):
                wide[j][pl.ds(e, NB, stride=16), :] = one[:, j * 128 : (j + 1) * 128]

        for j in range(2):
            lanes = pl.ds(j * 128, 128)
            ige[:, :, lanes] = wide[j][...].astype(BF16).reshape(NB, 16, 128)

        for turn in range(2):
            part = xc // 4 if turn else 1 - xc // 4

            @pl.when(inset)
            def _(turn=turn, part=part):
                src, dst, _ = back_to(part, ctx, slot)
                near(src, dst, IG0 + turn).start()

            @pl.when(jnp.logical_not(inset))
            def _(turn=turn, part=part):
                src, dst, device = back_to(part, ctx, slot)
                remote(src, dst, IG0 + turn, device).start()

            @pl.loop(1, 128)
            def _(step, turn=turn, part=part):
                src, dst, device = back_to(
                    part, lax.rem(ctx + step // HALF, NCTX), lax.rem(slot + step, HALF)
                )
                remote(src, dst, IG0 + turn, device).start()

        near(*column_share(level), PART2).wait()
        finish(part_col.at[pl.ds(0, 7)], PART2)
        part_sum[...] = jnp.sum(part_col[...], axis=0)
        near(part_sum, part_plane.at[level], PART3).start()

        @pl.loop(1, 8)
        def _(step):
            peer = lax.rem(level + step, 8)
            remote(part_sum, part_plane.at[level], PART3, column_dev(peer)).start()

        @pl.when(inset)
        def _():
            for part in range(2):
                src, dst, _ = inner_to(part, group, xq)
                near(src, dst, IN0 + part).wait()
                finish(ine.at[pl.ds(0, 127)], IN0 + part)

        @pl.when(jnp.logical_not(inset))
        def _():
            for part in range(2):
                finish(ine.at[pl.ds(0, 128)], IN0 + part)

        unpack(ine)

        @pl.loop(0, 16)
        def _(e):
            one = dot(mge_by[e], take(e), NT)
            gr[e] = jnp.where(keep_right, one, 0.0).astype(BF16)

    pl.run_scoped(
        columns,
        pltpu.VMEM((NB * 16, 128), F32),
        pltpu.VMEM((NB * 16, 128), F32),
        pltpu.VMEM((16, NB, 256), BF16),
    )

    def right_to(peer):
        return gr.at[pl.ds(peer * 2, 2)], gr_in.at[xc]

    near(*right_to(xc), GR).start()

    @pl.loop(1, 8)
    def _(step):
        peer = lax.rem(xc + step, 8)
        remote(*right_to(peer), GR, (ctx, zlo * 8 + peer)).start()

    near(part_sum, part_plane.at[level], PART3).wait()
    finish(part_plane.at[pl.ds(0, 7)], PART3)
    near(part_plane, part_all.at[plane], PART4).start()

    @pl.loop(1, 32)
    def _(step):
        peer = lax.rem(plane + step, 32)
        remote(part_plane, part_all.at[plane], PART4, plane_dev(peer)).start()

    def home_to(part, other):
        return (
            ret.at[part, pl.ds(al(other, CB), CB), :],
            home_ref.at[:, pl.ds(al(slot + HALF * part, BS), BS)],
        )

    for turn in range(2):
        part = half if turn else 1 - half

        @pl.when(inset)
        def _(turn=turn):
            src, dst, _ = back_to(xc // 4 if turn else 1 - xc // 4, ctx, slot)
            near(src, dst, IG0 + turn).wait()
            finish(ige.at[pl.ds(0, 127)], IG0 + turn)

        @pl.when(jnp.logical_not(inset))
        def _(turn=turn):
            finish(ige.at[pl.ds(0, 128)], IG0 + turn)

        ret[part] = dot(igx[part], lp[part], TN).astype(BF16)
        near(*home_to(part, slot), RET0 + turn).start()

        @pl.loop(1, HALF)
        def _(step, turn=turn, part=part):
            other = lax.rem(slot + step, HALF)
            remote(*home_to(part, other), RET0 + turn, (ctx, half * HALF + other)).start()

        if turn == 0:
            glp[...] = dot(igx[part], xp[part], NN).astype(BF16)
            bands(glp, glp_in, GL)

    own = dot(igx[half], xp[half], NN)

    near(part_plane, part_all.at[plane], PART4).wait()
    finish(part_all.at[pl.ds(0, 31)], PART4)
    flat = part_all.reshape(NB * 8, 128)
    for p in range(16):
        block = flat[pl.ds(p * CB, CB), :]
        gfirst_ref[2 * p] = block[:, :CB]
        gfirst_ref[2 * p + 1] = block[:, CB:]
    for k in range(KC):
        block = flat[pl.ds(1024 + k, CG, stride=KC), :]
        for i in range(CB // KC):
            gsecond_ref[i * KC + k] = block[:, i * CG : (i + 1) * CG]

    near(*right_to(xc), GR).wait()
    finish(gr_in.at[pl.ds(0, 7)], GR)
    total = gr_in[0].astype(F32)
    for other in range(1, 8):
        total += gr_in[other].astype(F32)
    gright_ref[...] = total.astype(BF16)

    finish(glp_in.at[pl.ds(0, 320), :], GL)
    gleft_ref[0] = jnp.where(keep, own + glp_in[...].astype(F32), 0.0).astype(BF16)
    for turn in range(2):
        near(*home_to(half if turn else 1 - half, slot), RET0 + turn).wait()
        finish(ret.at[0, pl.ds(0, (HALF - 1) * CB), :], RET0 + turn)


def on_device(inputs, mixed, grad_out, left_weight, right_weight, first_weight, second_weight):
    home, grad_left, grad_right, grad_first, grad_second = pl.pallas_call(
        kernel,
        out_shape=[
            jax.ShapeDtypeStruct((CB, NCHAN * BS), BF16),
            jax.ShapeDtypeStruct((1, BS, BS), BF16),
            jax.ShapeDtypeStruct((2, NB, NB), BF16),
            jax.ShapeDtypeStruct((CG, CB, CB), F32),
            jax.ShapeDtypeStruct((CB, CG, CG), F32),
        ],
        in_specs=[ANY] * 5 + [VMEM] * 2,
        out_specs=[ANY] + [VMEM] * 4,
        scratch_shapes=[
            pltpu.VMEM((D, BS), BF16),
            pltpu.VMEM((D, BS), BF16),
            pltpu.VMEM((2, HALF * CB, BS), BF16),
            pltpu.VMEM((2, BS, BS), BF16),
            pltpu.VMEM((16, NB, NB), BF16),
            pltpu.VMEM((2, BS, HALF * CB), BF16),
            pltpu.VMEM((BS, D), BF16),
            pltpu.VMEM((NB, 16, 256), BF16),
            pltpu.VMEM((NB, 16, 256), BF16),
            pltpu.VMEM((2048, 128), F32),
            pltpu.VMEM((32, 64, 128), F32),
            pltpu.VMEM((64, 128), F32),
            pltpu.VMEM((8, 8, 128), F32),
            pltpu.VMEM((8, 128), F32),
            pltpu.VMEM((8, 8, 128), F32),
            pltpu.VMEM((32, 8, 8, 128), F32),
            pltpu.VMEM((NB, 16, 256), BF16),
            pltpu.VMEM((2, BS, HALF * CB), BF16),
            pltpu.VMEM((16, NB, NB), BF16),
            pltpu.VMEM((8, 2, NB, NB), BF16),
            pltpu.VMEM((2, HALF * CB, BS), BF16),
            pltpu.VMEM((BS, BS), BF16),
            pltpu.VMEM((BS, BS), BF16),
            pltpu.SemaphoreType.DMA((SEMS,)),
            pltpu.SemaphoreType.DMA((SEMS,)),
            pltpu.SemaphoreType.DMA((SEMS,)),
            pltpu.SemaphoreType.REGULAR,
        ],
        compiler_params=pltpu.CompilerParams(
            collective_id=1, has_side_effects=True, vmem_limit_bytes=62 * 1024 * 1024
        ),
        name="layer",
    )(inputs, mixed, grad_out, left_weight, right_weight, first_weight, second_weight)
    grad_input = (grad_out.astype(F32) + home.astype(F32)).astype(BF16)
    return (grad_input, grad_left, grad_right, grad_first, grad_second)


def solution(mesh):
    in_specs = (
        P("chan", "ctx"),
        P("chan", "ctx"),
        P("chan", "ctx"),
        P(("ctx", "chan"), None, None),
        P(("ctx", "chan"), None, None),
        P(),
        P(),
    )
    out_specs = (
        P("chan", "ctx"),
        P(("ctx", "chan"), None, None),
        P(("ctx", "chan"), None, None),
        P(),
        P(),
    )
    return jax.shard_map(
        on_device, mesh=mesh, in_specs=in_specs, out_specs=out_specs, check_vma=False
    )
```

```python
import jax
import jax.numpy as jnp
from jax import lax
from jax.experimental import pallas as pl
from jax.experimental.pallas import tpu as pltpu
from jax.sharding import PartitionSpec as P

MESH = pl.DeviceIdType.MESH
ANY = pl.BlockSpec(memory_space=pl.ANY)
VMEM = pl.BlockSpec(memory_space=pltpu.VMEM)
NCTX, NCHAN, NDEV, HALF = 8, 32, 256, 16
BS, CB, CG, NB, D = 512, 64, 32, 256, 2048
KC = 16
F32, BF16 = jnp.float32, jnp.bfloat16
NN, NT, TN = ((1,), (0,)), ((1,), (1,)), ((0,), (0,))
LEFT, X0, X1, Y, G, RIGHT, IN0, IN1, MIX, PART1, IG0, IG1, GR, PART2, PART3, PART4, RET0, RET1, GL = range(19)
SEMS = 19


def dot(a, b, dims, precision=None):
    return lax.dot_general(a, b, (dims, ((), ())), preferred_element_type=F32, precision=precision)


def al(value, size):
    return pl.multiple_of(value * size, size)


def iota(shape, axis):
    return lax.broadcasted_iota(jnp.int32, shape, axis)


def kernel(
    x_ref, y_ref, g_ref, left_ref, right_ref, first_ref, second_ref,
    home_ref, gleft_ref, gright_ref, gfirst_ref, gsecond_ref,
    yt, gt, xp, lp, r16, inner, mg, mge, ine, parts, parts_in, part_own, part_col, part_sum, part_plane, part_all,
    ige, igx, gr, gr_in, ret, glp, glp_in, order,
    send, recv, local, ready,
):
    ctx, chan = lax.axis_index("ctx"), lax.axis_index("chan")
    half, slot = chan // HALF, lax.rem(chan, HALF)
    yy, zhi, zlo, xc = ctx // 2, lax.rem(ctx, 2), chan // 8, lax.rem(chan, 8)
    me = ctx * NCHAN + chan
    group = zhi * 16 + zlo * 4 + xc // 2
    member = yy * 2 + lax.rem(xc, 2)
    quarter_me = lax.rem(member, 4)
    hq = lax.rem(member // 4 + half, 2)
    inset = hq == half
    partner = (ctx, lax.rem(chan + HALF, NCHAN))
    plane, level = yy * 8 + xc, zhi * 4 + zlo

    def group_dev(one_group, one_member):
        other_ctx = one_member // 2 * 2 + one_group // 16
        level4 = lax.rem(one_group, 16) // 4
        return (other_ctx, level4 * 8 + lax.rem(one_group, 4) * 2 + lax.rem(one_member, 2))

    def remote(src, dst, index, device):
        return pltpu.make_async_remote_copy(
            src_ref=src, dst_ref=dst, send_sem=send.at[index], recv_sem=recv.at[index],
            device_id=device, device_id_type=MESH,
        )

    def finish(area, index):
        remote(area, area, index, partner).wait()

    def near(src, dst, index):
        return pltpu.make_async_copy(src, dst, local.at[index])

    barrier = pltpu.get_barrier_semaphore()

    def greet(semaphore, count, device_of):
        @pl.loop(1, count)
        def _(step):
            pl.semaphore_signal(
                semaphore, inc=1, device_id=device_of(step), device_id_type=MESH
            )

    def across(step):
        return (lax.rem(ctx + step, NCTX), chan)

    greet(barrier, NCHAN, lambda step: (ctx, lax.rem(chan + step, NCHAN)))
    greet(barrier, NCTX, across)
    pl.semaphore_wait(barrier, NCHAN + NCTX - 2)
    greet(ready, NCTX, across)

    def paired(part, other):
        return (
            x_ref.at[:, pl.ds(al(other + HALF * part, BS), BS)],
            xp.at[part, pl.ds(al(slot, CB), CB), :],
        )

    def whole(src, dst, peer):
        return src.at[:, pl.ds(al(peer, BS), BS)], dst.at[pl.ds(al(chan, CB), CB), :]

    def bands(src, dst, index):
        for band in range(4):
            area = (pl.ds(band * 128, 128), pl.ds(0, band * 128 + 128))
            remote(src.at[area], dst.at[area], index, partner).start()

    bands(left_ref.at[0], lp.at[half], LEFT)
    begin = [
        near(left_ref.at[0], lp.at[half], LEFT),
        near(*paired(0, slot), X0),
        near(*paired(1, slot), X1),
        near(*whole(y_ref, yt, chan), Y),
        near(*whole(g_ref, gt, chan), G),
        near(right_ref, r16.at[pl.ds(member * 2, 2)], RIGHT),
    ]
    for copy in begin:
        copy.start()

    @pl.loop(1, NCHAN)
    def _(step):
        peer = lax.rem(chan + step * 11, NCHAN)
        remote(*whole(y_ref, yt, peer), Y, (ctx, peer)).start()

        @pl.when(step < HALF)
        def _():
            other = lax.rem(slot + step, HALF)
            for part in range(2):
                remote(*paired(part, other), X0 + part, (ctx, half * HALF + other)).start()

    @pl.loop(1, NCHAN)
    def _(step):
        peer = lax.rem(chan + step * 11, NCHAN)
        remote(*whole(g_ref, gt, peer), G, (ctx, peer)).start()

    pl.semaphore_wait(ready, NCTX - 1)

    @pl.loop(1, 8)
    def _(step):
        device = group_dev(group, lax.rem(member + step, 8))
        remote(right_ref, r16.at[pl.ds(member * 2, 2)], RIGHT, device).start()

    for copy in begin:
        copy.wait()

    finish(lp.at[0, pl.ds(0, 320), :], LEFT)
    for part in range(2):
        finish(xp.at[part, pl.ds(0, (HALF - 1) * CB), :], X0 + part)
    keep = iota((BS, BS), 0) >= iota((BS, BS), 1)
    place, position = iota((BS, BS), 0), iota((BS, BS), 1)
    p_group, p_member = place // 16, lax.rem(place, 16) // 2
    owner = p_member // 2 * 64 + p_group // 16 * 32 + lax.rem(p_group, 16) // 4 * 8
    owner += lax.rem(p_group, 4) * 2 + lax.rem(p_member, 2)
    order[...] = (position == owner * 2 + lax.rem(place, 2)).astype(BF16)
    for part in range(2):
        lower = jnp.where(keep, lp[part], jnp.zeros((BS, BS), BF16))
        lower = dot(order[...], lower, NN).astype(BF16)
        lp[part] = lower
        inner[part] = dot(lower, xp[part], NT).astype(BF16)

    def inner_to(part, other_group, quarter):
        src = inner.at[part, pl.ds(al(other_group, 16), 16), pl.ds(al(quarter, 256), 256)]
        dst = ine.at[ctx * NCHAN + slot + HALF * part]
        turn = lax.rem(half + lax.rem(other_group, 16) // 8, 2)
        return src, dst, group_dev(other_group, turn * 4 + quarter)

    def inner_send(part):
        @pl.when(inset)
        def _():
            src, dst, _ = inner_to(part, group, quarter_me)
            near(src, dst, IN0 + part).start()

        @pl.when(jnp.logical_not(inset))
        def _():
            src, dst, device = inner_to(part, group, quarter_me)
            remote(src, dst, IN0 + part, device).start()

        @pl.loop(1, 128)
        def _(step):
            src, dst, device = inner_to(
                part, lax.rem(group + step // 4, 32), lax.rem(quarter_me + step, 4)
            )
            remote(src, dst, IN0 + part, device).start()

    def channel(w, s, fs, fg, gated):
        rows4, cols4 = iota((256, 256), 0), iota((256, 256), 1)
        same = (rows4 // CB) == (cols4 // CB)
        spread4 = (lax.rem(iota((CB, 256), 1), CB) == iota((CB, 256), 0)).astype(BF16)
        for q in range(8):
            tall = first_ref[pl.ds(q * 4, 4)].reshape(256, CB)
            w[q] = jnp.where(same, dot(tall, spread4, NN), 0.0).astype(BF16)
        row, col = iota((BS, BS), 0), iota((BS, BS), 1)
        sec = second_ref[...].reshape(CG * CG, CB)
        own_out = iota((BS, CG * CG), 0) // KC == iota((BS, CG * CG), 1) // CG
        own_in = (lax.rem(iota((CG * CG, BS), 0), CG) == iota((CG * CG, BS), 1) // KC).astype(BF16)
        for i in range(CB // KC):
            unit = iota((BS, CB), 1) == i * KC + lax.rem(iota((BS, CB), 0), KC)
            wide = jnp.where(own_out, dot(unit.astype(BF16), sec, NT), 0.0).astype(BF16)
            wide = dot(wide, own_in, NN)
            s[i] = jnp.where(lax.rem(row, KC) == lax.rem(col, KC), wide, 0.0).astype(BF16)

        finish(yt.at[pl.ds(0, (NCHAN - 1) * CB), :], Y)
        for q in range(8):
            section = dot(w[q], yt[pl.ds(q * 256, 256), :], NN).astype(BF16)
            fs[pl.ds(q * 4, 4)] = section.reshape(4, CB, BS)
        finish(gt.at[pl.ds(0, (NCHAN - 1) * CB), :], G)

        inner_send(0)
        y3, g3 = yt.reshape(CG, CB, BS), gt.reshape(CG, CB, BS)
        lane = iota((BS, 128), 1)
        source = iota((BS, 128), 0) // KC
        second = jnp.zeros((BS, 128), F32)
        for i in range(CB // KC):
            cols = pl.ds(i * KC, KC)
            section = fs[:, cols, :].reshape(BS, BS)
            pre = dot(s[i], section, NN)
            y = y3[:, cols, :].reshape(BS, BS).astype(F32)
            g = g3[:, cols, :].reshape(BS, BS).astype(F32)
            sig = jax.nn.sigmoid(pre)
            gsig = g * sig
            gg = (gsig * y * (1.0 + pre * (1.0 - sig))).astype(BF16)
            gated[:, cols, :] = (gsig * pre).reshape(CG, KC, BS)
            fg[:, cols, :] = dot(s[i], gg, TN).astype(BF16).reshape(CG, KC, BS)
            both = dot(gg, section, NT)
            both = jnp.where(lax.rem(row, KC) == lax.rem(col, KC), both, 0.0)
            pick = (lane == source + CG * i).astype(F32)
            second += dot(both, pick, NN, lax.Precision.HIGHEST)
        parts[pl.ds(1024, 512), :] = second
        parts[pl.ds(1536, 512), :] = jnp.zeros((512, 128), F32)
        left_lane = iota((CB, 128), 1) < CB
        for q in range(8):
            quad = pl.ds(q * 4, 4)
            fgq = fg[quad].reshape(256, BS)
            back = dot(w[q], fgq, TN)
            grad = (gated[quad].reshape(256, BS) + back).astype(BF16)
            mg[:, pl.ds(q * 256, 256)] = dot(order[...], grad, NT).astype(BF16)
            pf = dot(fgq, yt[pl.ds(q * 256, 256), :], NT)
            for a in range(2):
                one = pf[a * 128 : a * 128 + CB, a * 128 : a * 128 + 128]
                two = pf[a * 128 + CB : a * 128 + 128, a * 128 : a * 128 + 128]
                parts[pl.ds((q * 2 + a) * CB, CB), :] = jnp.where(left_lane, one, two)

    pl.run_scoped(
        channel,
        pltpu.VMEM((8, 256, 256), BF16),
        pltpu.VMEM((CB // KC, BS, BS), BF16),
        pltpu.VMEM((CG, CB, BS), BF16),
        pltpu.VMEM((CG, CB, BS), BF16),
        pltpu.VMEM((CG, CB, BS), F32),
    )

    def mixed_to(peer):
        other_group, other = peer // 8, lax.rem(peer, 8)
        eighth = lax.rem(other + lax.rem(other_group, 16) // 8 * 4, 8)
        src = mg.at[pl.ds(al(other_group, 16), 16), pl.ds(al(eighth, 256), 256)]
        return src, mge.at[me], group_dev(other_group, other)

    here = group * 8 + member
    near(*mixed_to(here)[:2], MIX).start()

    @pl.loop(1, NDEV)
    def _(step):
        src, dst, device = mixed_to(lax.rem(here + step, NDEV))
        remote(src, dst, MIX, device).start()

    def plane_dev(peer):
        return ((peer // 8) * 2 + zhi, zlo * 8 + lax.rem(peer, 8))

    def column_dev(peer):
        return (yy * 2 + peer // 4, lax.rem(peer, 4) * 8 + xc)

    def share(peer):
        return parts.at[pl.ds(al(peer, 64), 64), :], parts_in.at[plane]

    near(*share(plane), PART1).start()

    @pl.loop(1, 32)
    def _(step):
        peer = lax.rem(plane + step, 32)
        remote(*share(peer), PART1, plane_dev(peer)).start()

    inner_send(1)
    near(*share(plane), PART1).wait()
    finish(parts_in.at[pl.ds(0, 31)], PART1)
    part_own[...] = jnp.sum(parts_in[...], axis=0)

    def column_share(peer):
        return part_own.at[pl.ds(al(peer, 8), 8), :], part_col.at[level]

    near(*column_share(level), PART2).start()

    @pl.loop(1, 8)
    def _(step):
        peer = lax.rem(level + step, 8)
        remote(*column_share(peer), PART2, column_dev(peer)).start()

    keep_right = iota((NB, NB), 0) >= iota((NB, NB), 1)
    finish(r16.at[pl.ds(0, 14)], RIGHT)

    @pl.loop(0, 16)
    def _(e):
        r16[e] = jnp.where(keep_right, r16[e], jnp.zeros((NB, NB), BF16)).T

    def back_to(part, other_ctx, other_slot):
        src = ige.at[other_ctx * NCHAN + other_slot + HALF * part]
        dst = igx.at[part, pl.ds(al(group, 16), 16), pl.ds(al(quarter_me, 256), 256)]
        return src, dst, (other_ctx, hq * HALF + other_slot)

    def columns(wide0, wide1, mge_by):
        wide = (wide0, wide1)

        def unpack(ref):
            for j in range(2):
                lanes = pl.ds(j * 128, 128)
                wide[j][...] = ref[:, :, lanes].reshape(NB * 16, 128).astype(F32)

        def take(e):
            rows = pl.ds(e, NB, stride=16)
            return jnp.concatenate([w[rows, :] for w in wide], axis=1).astype(BF16)

        near(*mixed_to(here)[:2], MIX).wait()
        finish(mge.at[pl.ds(0, NDEV - 1)], MIX)
        unpack(mge)

        @pl.loop(0, 16, unroll=2)
        def _(e):
            mge_by[e] = take(e)

        @pl.loop(0, 16, unroll=2)
        def _(e):
            one = dot(r16[e], mge_by[e], NN)
            for j in range(2):
                wide[j][pl.ds(e, NB, stride=16), :] = one[:, j * 128 : (j + 1) * 128]

        for j in range(2):
            lanes = pl.ds(j * 128, 128)
            ige[:, :, lanes] = wide[j][...].astype(BF16).reshape(NB, 16, 128)

        for turn in range(2):
            part = hq if turn else 1 - hq

            @pl.when(inset)
            def _(turn=turn, part=part):
                src, dst, _ = back_to(part, ctx, slot)
                near(src, dst, IG0 + turn).start()

            @pl.when(jnp.logical_not(inset))
            def _(turn=turn, part=part):
                src, dst, device = back_to(part, ctx, slot)
                remote(src, dst, IG0 + turn, device).start()

            @pl.loop(1, 128)
            def _(step, turn=turn, part=part):
                src, dst, device = back_to(
                    part, lax.rem(ctx + step // HALF, NCTX), lax.rem(slot + step, HALF)
                )
                remote(src, dst, IG0 + turn, device).start()

        near(*column_share(level), PART2).wait()
        finish(part_col.at[pl.ds(0, 7)], PART2)
        part_sum[...] = jnp.sum(part_col[...], axis=0)
        near(part_sum, part_plane.at[level], PART3).start()

        @pl.loop(1, 8)
        def _(step):
            peer = lax.rem(level + step, 8)
            remote(part_sum, part_plane.at[level], PART3, column_dev(peer)).start()

        @pl.when(inset)
        def _():
            for part in range(2):
                src, dst, _ = inner_to(part, group, quarter_me)
                near(src, dst, IN0 + part).wait()
                finish(ine.at[pl.ds(0, 127)], IN0 + part)

        @pl.when(jnp.logical_not(inset))
        def _():
            for part in range(2):
                finish(ine.at[pl.ds(0, 128)], IN0 + part)

        unpack(ine)

        @pl.loop(0, 16, unroll=2)
        def _(e):
            one = dot(mge_by[e], take(e), NT)
            gr[e] = jnp.where(keep_right, one, 0.0).astype(BF16)

    pl.run_scoped(
        columns,
        pltpu.VMEM((NB * 16, 128), F32),
        pltpu.VMEM((NB * 16, 128), F32),
        pltpu.VMEM((16, NB, 256), BF16),
    )

    def right_to(peer):
        return gr.at[pl.ds(peer * 2, 2)], gr_in.at[member]

    near(*right_to(member), GR).start()

    @pl.loop(1, 8)
    def _(step):
        peer = lax.rem(member + step, 8)
        remote(*right_to(peer), GR, group_dev(group, peer)).start()

    near(part_sum, part_plane.at[level], PART3).wait()
    finish(part_plane.at[pl.ds(0, 7)], PART3)
    near(part_plane, part_all.at[plane], PART4).start()

    @pl.loop(1, 32)
    def _(step):
        peer = lax.rem(plane + step, 32)
        remote(part_plane, part_all.at[plane], PART4, plane_dev(peer)).start()

    def home_to(part, other):
        return (
            ret.at[part, pl.ds(al(other, CB), CB), :],
            home_ref.at[:, pl.ds(al(slot + HALF * part, BS), BS)],
        )

    for turn in range(2):
        part = half if turn else 1 - half

        @pl.when(inset)
        def _(turn=turn):
            src, dst, _ = back_to(hq if turn else 1 - hq, ctx, slot)
            near(src, dst, IG0 + turn).wait()
            finish(ige.at[pl.ds(0, 127)], IG0 + turn)

        @pl.when(jnp.logical_not(inset))
        def _(turn=turn):
            finish(ige.at[pl.ds(0, 128)], IG0 + turn)

        for step in range(4):
            quad = lax.rem(slot // 4 + step, 4)
            area = pl.ds(al(quad, 256), 256)
            ret[part, area, :] = dot(igx[part, :, area], lp[part], TN).astype(BF16)

            @pl.loop(0, 4)
            def _(last, turn=turn, part=part, quad=quad):
                other = quad * 4 + lax.rem(slot + last, 4)

                @pl.when(other == slot)
                def _():
                    near(*home_to(part, slot), RET0 + turn).start()

                @pl.when(other != slot)
                def _():
                    device = (ctx, half * HALF + other)
                    remote(*home_to(part, other), RET0 + turn, device).start()

        sorted_back = dot(order[...], igx[part], TN).astype(BF16)
        if turn == 0:
            glp[...] = dot(sorted_back, xp[part], NN).astype(BF16)
            bands(glp, glp_in, GL)
        else:
            own = dot(sorted_back, xp[part], NN)

    near(part_plane, part_all.at[plane], PART4).wait()
    finish(part_all.at[pl.ds(0, 31)], PART4)
    flat = part_all.reshape(NB * 8, 128)
    for p in range(16):
        block = flat[pl.ds(p * CB, CB), :]
        gfirst_ref[2 * p] = block[:, :CB]
        gfirst_ref[2 * p + 1] = block[:, CB:]
    for k in range(KC):
        block = flat[pl.ds(1024 + k, CG, stride=KC), :]
        for i in range(CB // KC):
            gsecond_ref[i * KC + k] = block[:, i * CG : (i + 1) * CG]

    near(*right_to(member), GR).wait()
    finish(gr_in.at[pl.ds(0, 7)], GR)
    total = gr_in[0].astype(F32)
    for other in range(1, 8):
        total += gr_in[other].astype(F32)
    gright_ref[...] = total.astype(BF16)

    finish(glp_in.at[pl.ds(0, 320), :], GL)
    gleft_ref[0] = jnp.where(keep, own + glp_in[...].astype(F32), 0.0).astype(BF16)
    for turn in range(2):
        near(*home_to(half if turn else 1 - half, slot), RET0 + turn).wait()
        finish(ret.at[0, pl.ds(0, (HALF - 1) * CB), :], RET0 + turn)


def on_device(inputs, mixed, grad_out, left_weight, right_weight, first_weight, second_weight):
    home, grad_left, grad_right, grad_first, grad_second = pl.pallas_call(
        kernel,
        out_shape=[
            jax.ShapeDtypeStruct((CB, NCHAN * BS), BF16),
            jax.ShapeDtypeStruct((1, BS, BS), BF16),
            jax.ShapeDtypeStruct((2, NB, NB), BF16),
            jax.ShapeDtypeStruct((CG, CB, CB), F32),
            jax.ShapeDtypeStruct((CB, CG, CG), F32),
        ],
        in_specs=[ANY] * 5 + [VMEM] * 2,
        out_specs=[ANY] + [VMEM] * 4,
        scratch_shapes=[
            pltpu.VMEM((D, BS), BF16),
            pltpu.VMEM((D, BS), BF16),
            pltpu.VMEM((2, HALF * CB, BS), BF16),
            pltpu.VMEM((2, BS, BS), BF16),
            pltpu.VMEM((16, NB, NB), BF16),
            pltpu.VMEM((2, BS, HALF * CB), BF16),
            pltpu.VMEM((BS, D), BF16),
            pltpu.VMEM((NB, 16, 256), BF16),
            pltpu.VMEM((NB, 16, 256), BF16),
            pltpu.VMEM((2048, 128), F32),
            pltpu.VMEM((32, 64, 128), F32),
            pltpu.VMEM((64, 128), F32),
            pltpu.VMEM((8, 8, 128), F32),
            pltpu.VMEM((8, 128), F32),
            pltpu.VMEM((8, 8, 128), F32),
            pltpu.VMEM((32, 8, 8, 128), F32),
            pltpu.VMEM((NB, 16, 256), BF16),
            pltpu.VMEM((2, BS, HALF * CB), BF16),
            pltpu.VMEM((16, NB, NB), BF16),
            pltpu.VMEM((8, 2, NB, NB), BF16),
            pltpu.VMEM((2, HALF * CB, BS), BF16),
            pltpu.VMEM((BS, BS), BF16),
            pltpu.VMEM((BS, BS), BF16),
            pltpu.VMEM((BS, BS), BF16),
            pltpu.SemaphoreType.DMA((SEMS,)),
            pltpu.SemaphoreType.DMA((SEMS,)),
            pltpu.SemaphoreType.DMA((SEMS,)),
            pltpu.SemaphoreType.REGULAR,
        ],
        compiler_params=pltpu.CompilerParams(
            collective_id=1, has_side_effects=True, vmem_limit_bytes=62 * 1024 * 1024
        ),
        name="layer",
    )(
        inputs, mixed, grad_out, left_weight, right_weight, first_weight,
        jnp.transpose(second_weight, (1, 2, 0)),
    )
    grad_input = (grad_out.astype(F32) + home.astype(F32)).astype(BF16)
    return (grad_input, grad_left, grad_right, grad_first, grad_second)


def solution(mesh):
    in_specs = (
        P("chan", "ctx"),
        P("chan", "ctx"),
        P("chan", "ctx"),
        P(("ctx", "chan"), None, None),
        P(("ctx", "chan"), None, None),
        P(),
        P(),
    )
    out_specs = (
        P("chan", "ctx"),
        P(("ctx", "chan"), None, None),
        P(("ctx", "chan"), None, None),
        P(),
        P(),
    )
    return jax.shard_map(
        on_device, mesh=mesh, in_specs=in_specs, out_specs=out_specs, check_vma=False
    )
```

```python
import jax
import jax.numpy as jnp
from jax import lax
from jax.experimental import pallas as pl
from jax.experimental.pallas import tpu as pltpu
from jax.sharding import PartitionSpec as P

MESH = pl.DeviceIdType.MESH
ANY = pl.BlockSpec(memory_space=pl.ANY)
VMEM = pl.BlockSpec(memory_space=pltpu.VMEM)
NCTX, NCHAN, NDEV, HALF = 8, 32, 256, 16
BS, CB, CG, NB, D = 512, 64, 32, 256, 2048
KC = 16
F32, BF16 = jnp.float32, jnp.bfloat16
NN, NT, TN = ((1,), (0,)), ((1,), (1,)), ((0,), (0,))
LEFT, X0, X1, Y, G, RIGHT, IN0, IN1, MIX, PART1, IG0, IG1, GR, PART2, PART3, PART4, RET0, RET1, GL = range(19)
SEMS = 19


def dot(a, b, dims, precision=None):
    return lax.dot_general(a, b, (dims, ((), ())), preferred_element_type=F32, precision=precision)


def al(value, size):
    return pl.multiple_of(value * size, size)


def iota(shape, axis):
    return lax.broadcasted_iota(jnp.int32, shape, axis)


def kernel(
    x_ref, y_ref, g_ref, left_ref, right_ref, first_ref, second_ref,
    home_ref, gleft_ref, gright_ref, gfirst_ref, gsecond_ref,
    yt, gt, xp, lp, r16, inner, mg, mge, ine, parts, parts_in, part_own, part_col, part_sum, part_plane, part_all,
    ige, igx, gr, gr_in, ret, glp, glp_in, order,
    send, recv, local, ready,
):
    ctx, chan = lax.axis_index("ctx"), lax.axis_index("chan")
    half, slot = chan // HALF, lax.rem(chan, HALF)
    yy, zhi, zlo, xc = ctx // 2, lax.rem(ctx, 2), chan // 8, lax.rem(chan, 8)
    me = ctx * NCHAN + chan
    group = zhi * 16 + zlo * 4 + xc // 2
    member = yy * 2 + lax.rem(xc, 2)
    quarter_me = lax.rem(member, 4)
    hq = lax.rem(member // 4 + half, 2)
    inset = hq == half
    partner = (ctx, lax.rem(chan + HALF, NCHAN))
    plane, level = yy * 8 + xc, zhi * 4 + zlo

    def group_dev(one_group, one_member):
        other_ctx = one_member // 2 * 2 + one_group // 16
        level4 = lax.rem(one_group, 16) // 4
        return (other_ctx, level4 * 8 + lax.rem(one_group, 4) * 2 + lax.rem(one_member, 2))

    def remote(src, dst, index, device):
        return pltpu.make_async_remote_copy(
            src_ref=src, dst_ref=dst, send_sem=send.at[index], recv_sem=recv.at[index],
            device_id=device, device_id_type=MESH,
        )

    def finish(area, index):
        remote(area, area, index, partner).wait()

    def near(src, dst, index):
        return pltpu.make_async_copy(src, dst, local.at[index])

    barrier = pltpu.get_barrier_semaphore()

    def greet(semaphore, count, device_of):
        @pl.loop(1, count)
        def _(step):
            pl.semaphore_signal(
                semaphore, inc=1, device_id=device_of(step), device_id_type=MESH
            )

    def across(step):
        return (lax.rem(ctx + step, NCTX), chan)

    greet(barrier, NCHAN, lambda step: (ctx, lax.rem(chan + step, NCHAN)))
    greet(barrier, NCTX, across)
    pl.semaphore_wait(barrier, NCHAN + NCTX - 2)
    greet(ready, NCTX, across)

    def paired(part, other):
        return (
            x_ref.at[:, pl.ds(al(other + HALF * part, BS), BS)],
            xp.at[part, pl.ds(al(slot, CB), CB), :],
        )

    def whole(src, dst, peer):
        return src.at[:, pl.ds(al(peer, BS), BS)], dst.at[pl.ds(al(chan, CB), CB), :]

    def bands(src, dst, index):
        for band in range(4):
            area = (pl.ds(band * 128, 128), pl.ds(0, band * 128 + 128))
            remote(src.at[area], dst.at[area], index, partner).start()

    bands(left_ref.at[0], lp.at[half], LEFT)
    begin = [
        near(left_ref.at[0], lp.at[half], LEFT),
        near(*paired(0, slot), X0),
        near(*paired(1, slot), X1),
        near(*whole(y_ref, yt, chan), Y),
        near(*whole(g_ref, gt, chan), G),
        near(right_ref, r16.at[pl.ds(member * 2, 2)], RIGHT),
    ]
    for copy in begin:
        copy.start()

    @pl.loop(1, NCHAN)
    def _(step):
        peer = lax.rem(chan + step * 11, NCHAN)
        remote(*whole(y_ref, yt, peer), Y, (ctx, peer)).start()

        @pl.when(step < HALF)
        def _():
            other = lax.rem(slot + step, HALF)
            for part in range(2):
                remote(*paired(part, other), X0 + part, (ctx, half * HALF + other)).start()

    @pl.loop(1, NCHAN)
    def _(step):
        peer = lax.rem(chan + step * 11, NCHAN)
        remote(*whole(g_ref, gt, peer), G, (ctx, peer)).start()

    pl.semaphore_wait(ready, NCTX - 1)

    @pl.loop(1, 8)
    def _(step):
        device = group_dev(group, lax.rem(member + step, 8))
        remote(right_ref, r16.at[pl.ds(member * 2, 2)], RIGHT, device).start()

    for copy in begin:
        copy.wait()

    finish(lp.at[0, pl.ds(0, 320), :], LEFT)
    for part in range(2):
        finish(xp.at[part, pl.ds(0, (HALF - 1) * CB), :], X0 + part)
    keep = iota((BS, BS), 0) >= iota((BS, BS), 1)
    place, position = iota((BS, BS), 0), iota((BS, BS), 1)
    p_group, p_member = place // 16, lax.rem(place, 16) // 2
    owner = p_member // 2 * 64 + p_group // 16 * 32 + lax.rem(p_group, 16) // 4 * 8
    owner += lax.rem(p_group, 4) * 2 + lax.rem(p_member, 2)
    order[...] = (position == owner * 2 + lax.rem(place, 2)).astype(BF16)
    for part in range(2):
        lower = jnp.where(keep, lp[part], jnp.zeros((BS, BS), BF16))
        lower = dot(order[...], lower, NN).astype(BF16)
        lp[part] = lower
        inner[part] = dot(lower, xp[part], NT).astype(BF16)

    def inner_to(part, other_group, quarter):
        src = inner.at[part, pl.ds(al(other_group, 16), 16), pl.ds(al(quarter, 256), 256)]
        dst = ine.at[ctx * NCHAN + slot + HALF * part]
        turn = lax.rem(half + lax.rem(other_group, 16) // 8, 2)
        return src, dst, group_dev(other_group, turn * 4 + quarter)

    def inner_send(part):
        @pl.when(inset)
        def _():
            src, dst, _ = inner_to(part, group, quarter_me)
            near(src, dst, IN0 + part).start()

        @pl.when(jnp.logical_not(inset))
        def _():
            src, dst, device = inner_to(part, group, quarter_me)
            remote(src, dst, IN0 + part, device).start()

        @pl.loop(1, 128)
        def _(step):
            src, dst, device = inner_to(
                part, lax.rem(group + step // 4, 32), lax.rem(quarter_me + step, 4)
            )
            remote(src, dst, IN0 + part, device).start()

    def channel(w, s, fs, fg, gated):
        rows4, cols4 = iota((256, 256), 0), iota((256, 256), 1)
        same = (rows4 // CB) == (cols4 // CB)
        spread4 = (lax.rem(iota((CB, 256), 1), CB) == iota((CB, 256), 0)).astype(BF16)
        for q in range(8):
            tall = first_ref[pl.ds(q * 4, 4)].reshape(256, CB)
            w[q] = jnp.where(same, dot(tall, spread4, NN), 0.0).astype(BF16)
        row, col = iota((BS, BS), 0), iota((BS, BS), 1)
        sec = second_ref[...].reshape(CG * CG, CB)
        own_out = iota((BS, CG * CG), 0) // KC == iota((BS, CG * CG), 1) // CG
        own_in = (lax.rem(iota((CG * CG, BS), 0), CG) == iota((CG * CG, BS), 1) // KC).astype(BF16)
        for i in range(CB // KC):
            unit = iota((BS, CB), 1) == i * KC + lax.rem(iota((BS, CB), 0), KC)
            wide = jnp.where(own_out, dot(unit.astype(BF16), sec, NT), 0.0).astype(BF16)
            wide = dot(wide, own_in, NN)
            s[i] = jnp.where(lax.rem(row, KC) == lax.rem(col, KC), wide, 0.0).astype(BF16)

        finish(yt.at[pl.ds(0, (NCHAN - 1) * CB), :], Y)
        for q in range(8):
            section = dot(w[q], yt[pl.ds(q * 256, 256), :], NN).astype(BF16)
            fs[pl.ds(q * 4, 4)] = section.reshape(4, CB, BS)
        finish(gt.at[pl.ds(0, (NCHAN - 1) * CB), :], G)

        inner_send(0)
        y3, g3 = yt.reshape(CG, CB, BS), gt.reshape(CG, CB, BS)
        lane = iota((BS, 128), 1)
        source = iota((BS, 128), 0) // KC
        second = jnp.zeros((BS, 128), F32)
        for i in range(CB // KC):
            cols = pl.ds(i * KC, KC)
            section = fs[:, cols, :].reshape(BS, BS)
            pre = dot(s[i], section, NN)
            y = y3[:, cols, :].reshape(BS, BS).astype(F32)
            g = g3[:, cols, :].reshape(BS, BS).astype(F32)
            sig = jax.nn.sigmoid(pre)
            gsig = g * sig
            gg = (gsig * y * (1.0 + pre * (1.0 - sig))).astype(BF16)
            gated[:, cols, :] = (gsig * pre).reshape(CG, KC, BS)
            fg[:, cols, :] = dot(s[i], gg, TN).astype(BF16).reshape(CG, KC, BS)
            both = dot(gg, section, NT)
            both = jnp.where(lax.rem(row, KC) == lax.rem(col, KC), both, 0.0)
            pick = (lane == source + CG * i).astype(F32)
            second += dot(both, pick, NN, lax.Precision.HIGHEST)
        parts[pl.ds(1024, 512), :] = second
        parts[pl.ds(1536, 512), :] = jnp.zeros((512, 128), F32)
        left_lane = iota((CB, 128), 1) < CB
        for q in range(8):
            quad = pl.ds(q * 4, 4)
            fgq = fg[quad].reshape(256, BS)
            back = dot(w[q], fgq, TN)
            grad = (gated[quad].reshape(256, BS) + back).astype(BF16)
            mg[:, pl.ds(q * 256, 256)] = dot(order[...], grad, NT).astype(BF16)
            pf = dot(fgq, yt[pl.ds(q * 256, 256), :], NT)
            for a in range(2):
                one = pf[a * 128 : a * 128 + CB, a * 128 : a * 128 + 128]
                two = pf[a * 128 + CB : a * 128 + 128, a * 128 : a * 128 + 128]
                parts[pl.ds((q * 2 + a) * CB, CB), :] = jnp.where(left_lane, one, two)

    pl.run_scoped(
        channel,
        pltpu.VMEM((8, 256, 256), BF16),
        pltpu.VMEM((CB // KC, BS, BS), BF16),
        pltpu.VMEM((CG, CB, BS), BF16),
        pltpu.VMEM((CG, CB, BS), BF16),
        pltpu.VMEM((CG, CB, BS), F32),
    )

    def plane_dev(peer):
        return ((peer // 8) * 2 + zhi, zlo * 8 + lax.rem(peer, 8))

    def column_dev(peer):
        return (yy * 2 + peer // 4, lax.rem(peer, 4) * 8 + xc)

    def share(peer):
        return parts.at[pl.ds(al(peer, 64), 64), :], parts_in.at[plane]

    near(*share(plane), PART1).start()

    @pl.loop(1, 32)
    def _(step):
        peer = lax.rem(plane + step, 32)
        remote(*share(peer), PART1, plane_dev(peer)).start()

    def mixed_to(peer):
        other_group, other = peer // 8, lax.rem(peer, 8)
        eighth = lax.rem(other + lax.rem(other_group, 16) // 8 * 4, 8)
        src = mg.at[pl.ds(al(other_group, 16), 16), pl.ds(al(eighth, 256), 256)]
        return src, mge.at[me], group_dev(other_group, other)

    here = group * 8 + member
    near(*mixed_to(here)[:2], MIX).start()

    @pl.loop(1, NDEV)
    def _(step):
        src, dst, device = mixed_to(lax.rem(here + step, NDEV))
        remote(src, dst, MIX, device).start()

    near(*share(plane), PART1).wait()
    finish(parts_in.at[pl.ds(0, 31)], PART1)
    part_own[...] = jnp.sum(parts_in[...], axis=0)

    def column_share(peer):
        return part_own.at[pl.ds(al(peer, 8), 8), :], part_col.at[level]

    near(*column_share(level), PART2).start()

    @pl.loop(1, 8)
    def _(step):
        peer = lax.rem(level + step, 8)
        remote(*column_share(peer), PART2, column_dev(peer)).start()

    inner_send(1)

    keep_right = iota((NB, NB), 0) >= iota((NB, NB), 1)
    finish(r16.at[pl.ds(0, 14)], RIGHT)

    @pl.loop(0, 16)
    def _(e):
        r16[e] = jnp.where(keep_right, r16[e], jnp.zeros((NB, NB), BF16)).T

    def back_to(part, other_ctx, other_slot):
        src = ige.at[other_ctx * NCHAN + other_slot + HALF * part]
        dst = igx.at[part, pl.ds(al(group, 16), 16), pl.ds(al(quarter_me, 256), 256)]
        return src, dst, (other_ctx, hq * HALF + other_slot)

    def right_to(peer):
        return gr.at[pl.ds(peer * 2, 2)], gr_in.at[member]

    def columns(wide0, wide1, mge_by):
        wide = (wide0, wide1)

        def unpack(ref):
            for j in range(2):
                lanes = pl.ds(j * 128, 128)
                wide[j][...] = ref[:, :, lanes].reshape(NB * 16, 128).astype(F32)

        def take(e):
            rows = pl.ds(e, NB, stride=16)
            return jnp.concatenate([w[rows, :] for w in wide], axis=1).astype(BF16)

        near(*mixed_to(here)[:2], MIX).wait()
        finish(mge.at[pl.ds(0, NDEV - 1)], MIX)
        near(*column_share(level), PART2).wait()
        finish(part_col.at[pl.ds(0, 7)], PART2)
        part_sum[...] = jnp.sum(part_col[...], axis=0)
        near(part_sum, part_plane.at[level], PART3).start()

        @pl.loop(1, 8)
        def _(step):
            peer = lax.rem(level + step, 8)
            remote(part_sum, part_plane.at[level], PART3, column_dev(peer)).start()

        unpack(mge)

        @pl.loop(0, 16, unroll=2)
        def _(e):
            mge_by[e] = take(e)

        @pl.loop(0, 16, unroll=2)
        def _(e):
            one = dot(r16[e], mge_by[e], NN)
            for j in range(2):
                wide[j][pl.ds(e, NB, stride=16), :] = one[:, j * 128 : (j + 1) * 128]

        for j in range(2):
            lanes = pl.ds(j * 128, 128)
            ige[:, :, lanes] = wide[j][...].astype(BF16).reshape(NB, 16, 128)

        def back_send(turn):
            part = hq if turn else 1 - hq

            @pl.when(inset)
            def _(turn=turn, part=part):
                src, dst, _ = back_to(part, ctx, slot)
                near(src, dst, IG0 + turn).start()

            @pl.when(jnp.logical_not(inset))
            def _(turn=turn, part=part):
                src, dst, device = back_to(part, ctx, slot)
                remote(src, dst, IG0 + turn, device).start()

            @pl.loop(1, 128)
            def _(step, turn=turn, part=part):
                src, dst, device = back_to(
                    part, lax.rem(ctx + step // HALF, NCTX), lax.rem(slot + step, HALF)
                )
                remote(src, dst, IG0 + turn, device).start()

        back_send(0)
        near(part_sum, part_plane.at[level], PART3).wait()
        finish(part_plane.at[pl.ds(0, 7)], PART3)
        near(part_plane, part_all.at[plane], PART4).start()

        @pl.loop(1, 32)
        def _(step):
            peer = lax.rem(plane + step, 32)
            remote(part_plane, part_all.at[plane], PART4, plane_dev(peer)).start()

        back_send(1)

        @pl.when(inset)
        def _():
            for part in range(2):
                src, dst, _ = inner_to(part, group, quarter_me)
                near(src, dst, IN0 + part).wait()
                finish(ine.at[pl.ds(0, 127)], IN0 + part)

        @pl.when(jnp.logical_not(inset))
        def _():
            for part in range(2):
                finish(ine.at[pl.ds(0, 128)], IN0 + part)

        unpack(ine)

        @pl.loop(0, 16, unroll=2)
        def _(e):
            one = dot(mge_by[e], take(e), NT)
            gr[e] = jnp.where(keep_right, one, 0.0).astype(BF16)

        near(*right_to(member), GR).start()

        @pl.loop(1, 8)
        def _(step):
            peer = lax.rem(member + step, 8)
            remote(*right_to(peer), GR, group_dev(group, peer)).start()

    pl.run_scoped(
        columns,
        pltpu.VMEM((NB * 16, 128), F32),
        pltpu.VMEM((NB * 16, 128), F32),
        pltpu.VMEM((16, NB, 256), BF16),
    )

    def home_to(part, other):
        return (
            ret.at[part, pl.ds(al(other, CB), CB), :],
            home_ref.at[:, pl.ds(al(slot + HALF * part, BS), BS)],
        )

    for turn in range(2):
        part = half if turn else 1 - half

        @pl.when(inset)
        def _(turn=turn):
            src, dst, _ = back_to(hq if turn else 1 - hq, ctx, slot)
            near(src, dst, IG0 + turn).wait()
            finish(ige.at[pl.ds(0, 127)], IG0 + turn)

        @pl.when(jnp.logical_not(inset))
        def _(turn=turn):
            finish(ige.at[pl.ds(0, 128)], IG0 + turn)

        if turn == 1:
            bands(glp, glp_in, GL)
        for step in range(4):
            quad = lax.rem(slot // 4 + step, 4)
            area = pl.ds(al(quad, 256), 256)
            ret[part, area, :] = dot(igx[part, :, area], lp[part], TN).astype(BF16)

            @pl.loop(0, 4)
            def _(last, turn=turn, part=part, quad=quad):
                other = quad * 4 + lax.rem(slot + last, 4)

                @pl.when(other == slot)
                def _():
                    near(*home_to(part, slot), RET0 + turn).start()

                @pl.when(other != slot)
                def _():
                    device = (ctx, half * HALF + other)
                    remote(*home_to(part, other), RET0 + turn, device).start()

        sorted_back = dot(order[...], igx[part], TN).astype(BF16)
        if turn == 0:
            glp[...] = dot(sorted_back, xp[part], NN).astype(BF16)
        else:
            own = dot(sorted_back, xp[part], NN)

    near(part_plane, part_all.at[plane], PART4).wait()
    finish(part_all.at[pl.ds(0, 31)], PART4)
    flat = part_all.reshape(NB * 8, 128)
    for p in range(16):
        block = flat[pl.ds(p * CB, CB), :]
        gfirst_ref[2 * p] = block[:, :CB]
        gfirst_ref[2 * p + 1] = block[:, CB:]
    for k in range(KC):
        block = flat[pl.ds(1024 + k, CG, stride=KC), :]
        for i in range(CB // KC):
            gsecond_ref[i * KC + k] = block[:, i * CG : (i + 1) * CG]

    near(*right_to(member), GR).wait()
    finish(gr_in.at[pl.ds(0, 7)], GR)
    total = gr_in[0].astype(F32)
    for other in range(1, 8):
        total += gr_in[other].astype(F32)
    gright_ref[...] = total.astype(BF16)

    finish(glp_in.at[pl.ds(0, 320), :], GL)
    gleft_ref[0] = jnp.where(keep, own + glp_in[...].astype(F32), 0.0).astype(BF16)
    for turn in range(2):
        near(*home_to(half if turn else 1 - half, slot), RET0 + turn).wait()
        finish(ret.at[0, pl.ds(0, (HALF - 1) * CB), :], RET0 + turn)


def on_device(inputs, mixed, grad_out, left_weight, right_weight, first_weight, second_weight):
    home, grad_left, grad_right, grad_first, grad_second = pl.pallas_call(
        kernel,
        out_shape=[
            jax.ShapeDtypeStruct((CB, NCHAN * BS), BF16),
            jax.ShapeDtypeStruct((1, BS, BS), BF16),
            jax.ShapeDtypeStruct((2, NB, NB), BF16),
            jax.ShapeDtypeStruct((CG, CB, CB), F32),
            jax.ShapeDtypeStruct((CB, CG, CG), F32),
        ],
        in_specs=[ANY] * 5 + [VMEM] * 2,
        out_specs=[ANY] + [VMEM] * 4,
        scratch_shapes=[
            pltpu.VMEM((D, BS), BF16),
            pltpu.VMEM((D, BS), BF16),
            pltpu.VMEM((2, HALF * CB, BS), BF16),
            pltpu.VMEM((2, BS, BS), BF16),
            pltpu.VMEM((16, NB, NB), BF16),
            pltpu.VMEM((2, BS, HALF * CB), BF16),
            pltpu.VMEM((BS, D), BF16),
            pltpu.VMEM((NB, 16, 256), BF16),
            pltpu.VMEM((NB, 16, 256), BF16),
            pltpu.VMEM((2048, 128), F32),
            pltpu.VMEM((32, 64, 128), F32),
            pltpu.VMEM((64, 128), F32),
            pltpu.VMEM((8, 8, 128), F32),
            pltpu.VMEM((8, 128), F32),
            pltpu.VMEM((8, 8, 128), F32),
            pltpu.VMEM((32, 8, 8, 128), F32),
            pltpu.VMEM((NB, 16, 256), BF16),
            pltpu.VMEM((2, BS, HALF * CB), BF16),
            pltpu.VMEM((16, NB, NB), BF16),
            pltpu.VMEM((8, 2, NB, NB), BF16),
            pltpu.VMEM((2, HALF * CB, BS), BF16),
            pltpu.VMEM((BS, BS), BF16),
            pltpu.VMEM((BS, BS), BF16),
            pltpu.VMEM((BS, BS), BF16),
            pltpu.SemaphoreType.DMA((SEMS,)),
            pltpu.SemaphoreType.DMA((SEMS,)),
            pltpu.SemaphoreType.DMA((SEMS,)),
            pltpu.SemaphoreType.REGULAR,
        ],
        compiler_params=pltpu.CompilerParams(
            collective_id=1, has_side_effects=True, vmem_limit_bytes=62 * 1024 * 1024
        ),
        name="layer",
    )(
        inputs, mixed, grad_out, left_weight, right_weight, first_weight,
        jnp.transpose(second_weight, (1, 2, 0)),
    )
    grad_input = (grad_out.astype(F32) + home.astype(F32)).astype(BF16)
    return (grad_input, grad_left, grad_right, grad_first, grad_second)


def solution(mesh):
    in_specs = (
        P("chan", "ctx"),
        P("chan", "ctx"),
        P("chan", "ctx"),
        P(("ctx", "chan"), None, None),
        P(("ctx", "chan"), None, None),
        P(),
        P(),
    )
    out_specs = (
        P("chan", "ctx"),
        P(("ctx", "chan"), None, None),
        P(("ctx", "chan"), None, None),
        P(),
        P(),
    )
    return jax.shard_map(
        on_device, mesh=mesh, in_specs=in_specs, out_specs=out_specs, check_vma=False
    )
```

```python
import jax
import jax.numpy as jnp
from jax import lax
from jax.experimental import pallas as pl
from jax.experimental.pallas import tpu as pltpu
from jax.sharding import PartitionSpec as P

MESH = pl.DeviceIdType.MESH
ANY = pl.BlockSpec(memory_space=pl.ANY)
VMEM = pl.BlockSpec(memory_space=pltpu.VMEM)
NCTX, NCHAN, NDEV, HALF = 8, 32, 256, 16
BS, CB, CG, NB, D = 512, 64, 32, 256, 2048
KC = 16
F32, BF16 = jnp.float32, jnp.bfloat16
NN, NT, TN = ((1,), (0,)), ((1,), (1,)), ((0,), (0,))
LEFT, X0, X1, Y, G, RIGHT, IN0, IN1, MIX, PART1, IG0, IG1, GR, PART2, PART3, PART4, RET0, RET1, GL = range(19)
SEMS = 19


def dot(a, b, dims, precision=None):
    return lax.dot_general(a, b, (dims, ((), ())), preferred_element_type=F32, precision=precision)


def al(value, size):
    return pl.multiple_of(value * size, size)


def iota(shape, axis):
    return lax.broadcasted_iota(jnp.int32, shape, axis)


def kernel(
    x_ref, y_ref, g_ref, left_ref, right_ref, first_ref, second_ref,
    home_ref, gleft_ref, gright_ref, gfirst_ref, gsecond_ref,
    yt, gt, xp, lp, r16, inner, mg, mge, ine, parts, parts_in, part_own, part_col, part_sum, part_plane, part_all,
    ige, igx, gr, gr_in, ret, glp, glp_in, order,
    send, recv, local, ready,
):
    ctx, chan = lax.axis_index("ctx"), lax.axis_index("chan")
    half, slot = chan // HALF, lax.rem(chan, HALF)
    yy, zhi, zlo, xc = ctx // 2, lax.rem(ctx, 2), chan // 8, lax.rem(chan, 8)
    me = ctx * NCHAN + chan
    group = zhi * 16 + zlo * 4 + xc // 2
    member = yy * 2 + lax.rem(xc, 2)
    quarter_me = lax.rem(member, 4)
    hq = lax.rem(member // 4 + half, 2)
    inset = hq == half
    partner = (ctx, lax.rem(chan + HALF, NCHAN))
    plane, level = yy * 8 + xc, zhi * 4 + zlo

    def group_dev(one_group, one_member):
        other_ctx = one_member // 2 * 2 + one_group // 16
        level4 = lax.rem(one_group, 16) // 4
        return (other_ctx, level4 * 8 + lax.rem(one_group, 4) * 2 + lax.rem(one_member, 2))

    def remote(src, dst, index, device):
        return pltpu.make_async_remote_copy(
            src_ref=src, dst_ref=dst, send_sem=send.at[index], recv_sem=recv.at[index],
            device_id=device, device_id_type=MESH,
        )

    def finish(area, index):
        remote(area, area, index, partner).wait()

    def near(src, dst, index):
        return pltpu.make_async_copy(src, dst, local.at[index])

    barrier = pltpu.get_barrier_semaphore()

    def greet(semaphore, count, device_of):
        @pl.loop(1, count)
        def _(step):
            pl.semaphore_signal(
                semaphore, inc=1, device_id=device_of(step), device_id_type=MESH
            )

    def across(step):
        return (lax.rem(ctx + step, NCTX), chan)

    greet(barrier, NCHAN, lambda step: (ctx, lax.rem(chan + step, NCHAN)))
    greet(barrier, NCTX, across)
    pl.semaphore_wait(barrier, NCHAN + NCTX - 2)
    greet(ready, NCTX, across)

    def paired(part, other):
        return (
            x_ref.at[:, pl.ds(al(other + HALF * part, BS), BS)],
            xp.at[part, pl.ds(al(slot, CB), CB), :],
        )

    def whole(src, dst, peer):
        return src.at[:, pl.ds(al(peer, BS), BS)], dst.at[pl.ds(al(chan, CB), CB), :]

    def bands(src, dst, index):
        for band in range(4):
            area = (pl.ds(band * 128, 128), pl.ds(0, band * 128 + 128))
            remote(src.at[area], dst.at[area], index, partner).start()

    bands(left_ref.at[0], lp.at[half], LEFT)
    begin = [
        near(left_ref.at[0], lp.at[half], LEFT),
        near(*paired(0, slot), X0),
        near(*paired(1, slot), X1),
        near(*whole(y_ref, yt, chan), Y),
        near(*whole(g_ref, gt, chan), G),
        near(right_ref, r16.at[pl.ds(member * 2, 2)], RIGHT),
    ]
    for copy in begin:
        copy.start()

    @pl.loop(1, NCHAN)
    def _(step):
        peer = lax.rem(chan + step * 11, NCHAN)
        remote(*whole(y_ref, yt, peer), Y, (ctx, peer)).start()

        @pl.when(step < HALF)
        def _():
            other = lax.rem(slot + step, HALF)
            for part in range(2):
                remote(*paired(part, other), X0 + part, (ctx, half * HALF + other)).start()

    @pl.loop(1, NCHAN)
    def _(step):
        peer = lax.rem(chan + step * 11, NCHAN)
        remote(*whole(g_ref, gt, peer), G, (ctx, peer)).start()

    pl.semaphore_wait(ready, NCTX - 1)

    @pl.loop(1, 8)
    def _(step):
        device = group_dev(group, lax.rem(member + step, 8))
        remote(right_ref, r16.at[pl.ds(member * 2, 2)], RIGHT, device).start()

    for copy in begin:
        copy.wait()

    finish(lp.at[0, pl.ds(0, 320), :], LEFT)
    for part in range(2):
        finish(xp.at[part, pl.ds(0, (HALF - 1) * CB), :], X0 + part)
    keep = iota((BS, BS), 0) >= iota((BS, BS), 1)
    place, position = iota((BS, BS), 0), iota((BS, BS), 1)
    p_group, p_member = place // 16, lax.rem(place, 16) // 2
    owner = p_member // 2 * 64 + p_group // 16 * 32 + lax.rem(p_group, 16) // 4 * 8
    owner += lax.rem(p_group, 4) * 2 + lax.rem(p_member, 2)
    order[...] = (position == owner * 2 + lax.rem(place, 2)).astype(BF16)
    for part in range(2):
        lower = jnp.where(keep, lp[part], jnp.zeros((BS, BS), BF16))
        lower = dot(order[...], lower, NN).astype(BF16)
        lp[part] = lower
        inner[part] = dot(lower, xp[part], NT).astype(BF16)

    def inner_to(part, other_group, quarter):
        src = inner.at[part, pl.ds(al(other_group, 16), 16), pl.ds(al(quarter, 256), 256)]
        dst = ine.at[ctx * NCHAN + slot + HALF * part]
        turn = lax.rem(half + lax.rem(other_group, 16) // 8, 2)
        return src, dst, group_dev(other_group, turn * 4 + quarter)

    def inner_send(part):
        @pl.when(inset)
        def _():
            src, dst, _ = inner_to(part, group, quarter_me)
            near(src, dst, IN0 + part).start()

        @pl.when(jnp.logical_not(inset))
        def _():
            src, dst, device = inner_to(part, group, quarter_me)
            remote(src, dst, IN0 + part, device).start()

        @pl.loop(1, 128)
        def _(step):
            src, dst, device = inner_to(
                part, lax.rem(group + step // 4, 32), lax.rem(quarter_me + step, 4)
            )
            remote(src, dst, IN0 + part, device).start()

    def channel(w, s, fs, fg, gated):
        rows4, cols4 = iota((256, 256), 0), iota((256, 256), 1)
        same = (rows4 // CB) == (cols4 // CB)
        spread4 = (lax.rem(iota((CB, 256), 1), CB) == iota((CB, 256), 0)).astype(BF16)
        for q in range(8):
            tall = first_ref[pl.ds(q * 4, 4)].reshape(256, CB)
            w[q] = jnp.where(same, dot(tall, spread4, NN), 0.0).astype(BF16)
        row, col = iota((BS, BS), 0), iota((BS, BS), 1)
        sec = second_ref[...].reshape(CG * CG, CB)
        own_out = iota((BS, CG * CG), 0) // KC == iota((BS, CG * CG), 1) // CG
        own_in = (lax.rem(iota((CG * CG, BS), 0), CG) == iota((CG * CG, BS), 1) // KC).astype(BF16)
        for i in range(CB // KC):
            unit = iota((BS, CB), 1) == i * KC + lax.rem(iota((BS, CB), 0), KC)
            wide = jnp.where(own_out, dot(unit.astype(BF16), sec, NT), 0.0).astype(BF16)
            wide = dot(wide, own_in, NN)
            s[i] = jnp.where(lax.rem(row, KC) == lax.rem(col, KC), wide, 0.0).astype(BF16)

        finish(yt.at[pl.ds(0, (NCHAN - 1) * CB), :], Y)
        for q in range(8):
            section = dot(w[q], yt[pl.ds(q * 256, 256), :], NN).astype(BF16)
            fs[pl.ds(q * 4, 4)] = section.reshape(4, CB, BS)
        finish(gt.at[pl.ds(0, (NCHAN - 1) * CB), :], G)

        inner_send(0)
        y3, g3 = yt.reshape(CG, CB, BS), gt.reshape(CG, CB, BS)
        lane = iota((BS, 128), 1)
        source = iota((BS, 128), 0) // KC
        second = jnp.zeros((BS, 128), F32)
        for i in range(CB // KC):
            cols = pl.ds(i * KC, KC)
            section = fs[:, cols, :].reshape(BS, BS)
            pre = dot(s[i], section, NN)
            y = y3[:, cols, :].reshape(BS, BS).astype(F32)
            g = g3[:, cols, :].reshape(BS, BS).astype(F32)
            sig = jax.nn.sigmoid(pre)
            gsig = g * sig
            gg = (gsig * y * (1.0 + pre * (1.0 - sig))).astype(BF16)
            gated[:, cols, :] = (gsig * pre).reshape(CG, KC, BS)
            fg[:, cols, :] = dot(s[i], gg, TN).astype(BF16).reshape(CG, KC, BS)
            both = dot(gg, section, NT)
            both = jnp.where(lax.rem(row, KC) == lax.rem(col, KC), both, 0.0)
            pick = (lane == source + CG * i).astype(F32)
            second += dot(both, pick, NN, lax.Precision.HIGHEST)
        parts[pl.ds(1024, 512), :] = second
        parts[pl.ds(1536, 512), :] = jnp.zeros((512, 128), F32)
        left_lane = iota((CB, 128), 1) < CB
        for q in range(8):
            quad = pl.ds(q * 4, 4)
            fgq = fg[quad].reshape(256, BS)
            back = dot(w[q], fgq, TN)
            grad = (gated[quad].reshape(256, BS) + back).astype(BF16)
            mg[:, pl.ds(q * 256, 256)] = dot(order[...], grad, NT).astype(BF16)
            pf = dot(fgq, yt[pl.ds(q * 256, 256), :], NT)
            for a in range(2):
                one = pf[a * 128 : a * 128 + CB, a * 128 : a * 128 + 128]
                two = pf[a * 128 + CB : a * 128 + 128, a * 128 : a * 128 + 128]
                parts[pl.ds((q * 2 + a) * CB, CB), :] = jnp.where(left_lane, one, two)

    pl.run_scoped(
        channel,
        pltpu.VMEM((8, 256, 256), BF16),
        pltpu.VMEM((CB // KC, BS, BS), BF16),
        pltpu.VMEM((CG, CB, BS), BF16),
        pltpu.VMEM((CG, CB, BS), BF16),
        pltpu.VMEM((CG, CB, BS), F32),
    )

    def plane_dev(peer):
        return ((peer // 8) * 2 + zhi, zlo * 8 + lax.rem(peer, 8))

    def column_dev(peer):
        return (yy * 2 + peer // 4, lax.rem(peer, 4) * 8 + xc)

    def share(peer):
        return parts.at[pl.ds(al(peer, 64), 64), :], parts_in.at[plane]

    near(*share(plane), PART1).start()

    @pl.loop(1, 32)
    def _(step):
        peer = lax.rem(plane + step, 32)
        remote(*share(peer), PART1, plane_dev(peer)).start()

    def mixed_to(peer):
        other_group, other = peer // 8, lax.rem(peer, 8)
        eighth = lax.rem(other + lax.rem(other_group, 16) // 8 * 4, 8)
        src = mg.at[pl.ds(al(other_group, 16), 16), pl.ds(al(eighth, 256), 256)]
        return src, mge.at[me], group_dev(other_group, other)

    here = group * 8 + member
    near(*mixed_to(here)[:2], MIX).start()

    @pl.loop(1, NDEV)
    def _(step):
        src, dst, device = mixed_to(lax.rem(here + step, NDEV))
        remote(src, dst, MIX, device).start()

    near(*share(plane), PART1).wait()
    finish(parts_in.at[pl.ds(0, 31)], PART1)
    part_own[...] = jnp.sum(parts_in[...], axis=0)

    def column_share(peer):
        return part_own.at[pl.ds(al(peer, 8), 8), :], part_col.at[level]

    near(*column_share(level), PART2).start()

    @pl.loop(1, 8)
    def _(step):
        peer = lax.rem(level + step, 8)
        remote(*column_share(peer), PART2, column_dev(peer)).start()

    inner_send(1)

    keep_right = iota((NB, NB), 0) >= iota((NB, NB), 1)
    finish(r16.at[pl.ds(0, 14)], RIGHT)

    @pl.loop(0, 16)
    def _(e):
        r16[e] = jnp.where(keep_right, r16[e], jnp.zeros((NB, NB), BF16)).T

    def back_to(part, other_ctx, other_slot):
        src = ige.at[other_ctx * NCHAN + other_slot + HALF * part]
        dst = igx.at[part, pl.ds(al(group, 16), 16), pl.ds(al(quarter_me, 256), 256)]
        return src, dst, (other_ctx, hq * HALF + other_slot)

    def right_to(peer):
        return gr.at[pl.ds(peer * 2, 2)], gr_in.at[member]

    def columns(wide0, wide1, mge_by):
        wide = (wide0, wide1)

        def unpack(ref):
            for j in range(2):
                lanes = pl.ds(j * 128, 128)
                wide[j][...] = ref[:, :, lanes].reshape(NB * 16, 128).astype(F32)

        def take(e):
            rows = pl.ds(e, NB, stride=16)
            return jnp.concatenate([w[rows, :] for w in wide], axis=1).astype(BF16)

        near(*mixed_to(here)[:2], MIX).wait()
        finish(mge.at[pl.ds(0, NDEV - 1)], MIX)
        near(*column_share(level), PART2).wait()
        finish(part_col.at[pl.ds(0, 7)], PART2)
        part_sum[...] = jnp.sum(part_col[...], axis=0)
        near(part_sum, part_plane.at[level], PART3).start()

        @pl.loop(1, 8)
        def _(step):
            peer = lax.rem(level + step, 8)
            remote(part_sum, part_plane.at[level], PART3, column_dev(peer)).start()

        unpack(mge)

        @pl.loop(0, 16, unroll=2)
        def _(e):
            mge_by[e] = take(e)

        @pl.loop(0, 16, unroll=2)
        def _(e):
            one = dot(r16[e], mge_by[e], NN)
            for j in range(2):
                wide[j][pl.ds(e, NB, stride=16), :] = one[:, j * 128 : (j + 1) * 128]

        for j in range(2):
            lanes = pl.ds(j * 128, 128)
            ige[:, :, lanes] = wide[j][...].astype(BF16).reshape(NB, 16, 128)

        def back_send(turn):
            part = hq if turn else 1 - hq

            @pl.when(inset)
            def _(turn=turn, part=part):
                src, dst, _ = back_to(part, ctx, slot)
                near(src, dst, IG0 + turn).start()

            @pl.when(jnp.logical_not(inset))
            def _(turn=turn, part=part):
                src, dst, device = back_to(part, ctx, slot)
                remote(src, dst, IG0 + turn, device).start()

            @pl.loop(1, 128)
            def _(step, turn=turn, part=part):
                src, dst, device = back_to(
                    part, lax.rem(ctx + step // HALF, NCTX), lax.rem(slot + step, HALF)
                )
                remote(src, dst, IG0 + turn, device).start()

        back_send(0)
        near(part_sum, part_plane.at[level], PART3).wait()
        finish(part_plane.at[pl.ds(0, 7)], PART3)
        near(part_plane, part_all.at[plane], PART4).start()

        @pl.loop(1, 32)
        def _(step):
            peer = lax.rem(plane + step, 32)
            remote(part_plane, part_all.at[plane], PART4, plane_dev(peer)).start()

        back_send(1)

        @pl.when(inset)
        def _():
            for part in range(2):
                src, dst, _ = inner_to(part, group, quarter_me)
                near(src, dst, IN0 + part).wait()
                finish(ine.at[pl.ds(0, 127)], IN0 + part)

        @pl.when(jnp.logical_not(inset))
        def _():
            for part in range(2):
                finish(ine.at[pl.ds(0, 128)], IN0 + part)

        unpack(ine)

        @pl.loop(0, 16, unroll=2)
        def _(e):
            one = dot(mge_by[e], take(e), NT)
            gr[e] = jnp.where(keep_right, one, 0.0).astype(BF16)

    pl.run_scoped(
        columns,
        pltpu.VMEM((NB * 16, 128), F32),
        pltpu.VMEM((NB * 16, 128), F32),
        pltpu.VMEM((16, NB, 256), BF16),
    )

    def home_to(part, other):
        return (
            ret.at[part, pl.ds(al(other, CB), CB), :],
            home_ref.at[:, pl.ds(al(slot + HALF * part, BS), BS)],
        )

    for turn in range(2):
        part = half if turn else 1 - half

        @pl.when(inset)
        def _(turn=turn):
            src, dst, _ = back_to(hq if turn else 1 - hq, ctx, slot)
            near(src, dst, IG0 + turn).wait()
            finish(ige.at[pl.ds(0, 127)], IG0 + turn)

        @pl.when(jnp.logical_not(inset))
        def _(turn=turn):
            finish(ige.at[pl.ds(0, 128)], IG0 + turn)

        if turn == 1:
            bands(glp, glp_in, GL)
        for step in range(4):
            quad = lax.rem(slot // 4 + step, 4)
            area = pl.ds(al(quad, 256), 256)
            ret[part, area, :] = dot(igx[part, :, area], lp[part], TN).astype(BF16)

            @pl.loop(0, 4)
            def _(last, turn=turn, part=part, quad=quad):
                other = quad * 4 + lax.rem(slot + last, 4)

                @pl.when(other == slot)
                def _():
                    near(*home_to(part, slot), RET0 + turn).start()

                @pl.when(other != slot)
                def _():
                    device = (ctx, half * HALF + other)
                    remote(*home_to(part, other), RET0 + turn, device).start()

        sorted_back = dot(order[...], igx[part], TN).astype(BF16)
        if turn == 0:
            near(*right_to(member), GR).start()

            @pl.loop(1, 8)
            def _(step):
                peer = lax.rem(member + step, 8)
                remote(*right_to(peer), GR, group_dev(group, peer)).start()

            glp[...] = dot(sorted_back, xp[part], NN).astype(BF16)
        else:
            own = dot(sorted_back, xp[part], NN)

    near(part_plane, part_all.at[plane], PART4).wait()
    finish(part_all.at[pl.ds(0, 31)], PART4)
    flat = part_all.reshape(NB * 8, 128)
    for p in range(16):
        block = flat[pl.ds(p * CB, CB), :]
        gfirst_ref[2 * p] = block[:, :CB]
        gfirst_ref[2 * p + 1] = block[:, CB:]
    for k in range(KC):
        block = flat[pl.ds(1024 + k, CG, stride=KC), :]
        for i in range(CB // KC):
            gsecond_ref[i * KC + k] = block[:, i * CG : (i + 1) * CG]

    near(*right_to(member), GR).wait()
    finish(gr_in.at[pl.ds(0, 7)], GR)
    total = gr_in[0].astype(F32)
    for other in range(1, 8):
        total += gr_in[other].astype(F32)
    gright_ref[...] = total.astype(BF16)

    finish(glp_in.at[pl.ds(0, 320), :], GL)
    gleft_ref[0] = jnp.where(keep, own + glp_in[...].astype(F32), 0.0).astype(BF16)
    for turn in range(2):
        near(*home_to(half if turn else 1 - half, slot), RET0 + turn).wait()
        finish(ret.at[0, pl.ds(0, (HALF - 1) * CB), :], RET0 + turn)


def on_device(inputs, mixed, grad_out, left_weight, right_weight, first_weight, second_weight):
    home, grad_left, grad_right, grad_first, grad_second = pl.pallas_call(
        kernel,
        out_shape=[
            jax.ShapeDtypeStruct((CB, NCHAN * BS), BF16),
            jax.ShapeDtypeStruct((1, BS, BS), BF16),
            jax.ShapeDtypeStruct((2, NB, NB), BF16),
            jax.ShapeDtypeStruct((CG, CB, CB), F32),
            jax.ShapeDtypeStruct((CB, CG, CG), F32),
        ],
        in_specs=[ANY] * 5 + [VMEM] * 2,
        out_specs=[ANY] + [VMEM] * 4,
        scratch_shapes=[
            pltpu.VMEM((D, BS), BF16),
            pltpu.VMEM((D, BS), BF16),
            pltpu.VMEM((2, HALF * CB, BS), BF16),
            pltpu.VMEM((2, BS, BS), BF16),
            pltpu.VMEM((16, NB, NB), BF16),
            pltpu.VMEM((2, BS, HALF * CB), BF16),
            pltpu.VMEM((BS, D), BF16),
            pltpu.VMEM((NB, 16, 256), BF16),
            pltpu.VMEM((NB, 16, 256), BF16),
            pltpu.VMEM((2048, 128), F32),
            pltpu.VMEM((32, 64, 128), F32),
            pltpu.VMEM((64, 128), F32),
            pltpu.VMEM((8, 8, 128), F32),
            pltpu.VMEM((8, 128), F32),
            pltpu.VMEM((8, 8, 128), F32),
            pltpu.VMEM((32, 8, 8, 128), F32),
            pltpu.VMEM((NB, 16, 256), BF16),
            pltpu.VMEM((2, BS, HALF * CB), BF16),
            pltpu.VMEM((16, NB, NB), BF16),
            pltpu.VMEM((8, 2, NB, NB), BF16),
            pltpu.VMEM((2, HALF * CB, BS), BF16),
            pltpu.VMEM((BS, BS), BF16),
            pltpu.VMEM((BS, BS), BF16),
            pltpu.VMEM((BS, BS), BF16),
            pltpu.SemaphoreType.DMA((SEMS,)),
            pltpu.SemaphoreType.DMA((SEMS,)),
            pltpu.SemaphoreType.DMA((SEMS,)),
            pltpu.SemaphoreType.REGULAR,
        ],
        compiler_params=pltpu.CompilerParams(
            collective_id=1, has_side_effects=True, vmem_limit_bytes=62 * 1024 * 1024
        ),
        name="layer",
    )(
        inputs, mixed, grad_out, left_weight, right_weight, first_weight,
        jnp.transpose(second_weight, (1, 2, 0)),
    )
    grad_input = (grad_out.astype(F32) + home.astype(F32)).astype(BF16)
    return (grad_input, grad_left, grad_right, grad_first, grad_second)


def solution(mesh):
    in_specs = (
        P("chan", "ctx"),
        P("chan", "ctx"),
        P("chan", "ctx"),
        P(("ctx", "chan"), None, None),
        P(("ctx", "chan"), None, None),
        P(),
        P(),
    )
    out_specs = (
        P("chan", "ctx"),
        P(("ctx", "chan"), None, None),
        P(("ctx", "chan"), None, None),
        P(),
        P(),
    )
    return jax.shard_map(
        on_device, mesh=mesh, in_specs=in_specs, out_specs=out_specs, check_vma=False
    )
```
